32 devices in a mesh: dom: 8 (over z, y), sub: 4 (over x, core).
Axes of the slice: x: 2, y: 2, z: 4, core: 2. Of those that a mesh axis runs over, the one named last changes fastest.
Arguments:
- positions: float32 [3, 65536], P(None, ('dom', 'sub')), may hold values from -6 to 6
- fixed_mask: int32 [65536], P(('dom', 'sub')), may hold values 0 or 1
- send_count: int32 [8, 4, 5, 4], P('dom', 'sub'), may hold values from 0 to 128, as said below
- send_list: int32 [8, 4, 5, 4, 128], P('dom', 'sub'), may hold values from 0 to 2047, as said below
- block_nodes: int32 [64, 4096], P(None, ('dom', 'sub')), may hold values from 0 to 4607, as said below
- tet_corners: int32 [4, 524288], P(None, ('dom', 'sub')), may hold values from 0 to 63, as said below
Outputs:
- smoothed: float32 [3, 65536], P(None, ('dom', 'sub'))
The draws below stay inside these ranges and needn't reach their ends.
Inputs may be any that keep to these rules, and one draw needn't show every extreme that they name: send_count[d, s, k, t] is the number of nodes that partition (d, s) sends to the partition at dom index (d + k - 2) modulo the dom axis's size and sub index t; it is zero for k = 2, t = s. send_list[d, s, k, t, j] for j below send_count[d, s, k, t] is the local index of an owned node of partition (d, s), sent to that neighbour's ghost slot (k, s, j); later entries are ignored. `block_nodes`: entries are local columns of the block's partition: below 2048 an owned node, else 2048 + (k * 4 + t) * 128 + j for a ghost slot whose j is below the sending partition's count. `tet_corners`: the four corners of a tetrahedron are distinct rows.
All inputs are finite; a program needn't handle non-finite values. No bound on the sum of `fixed_mask` on one device may be relied on, other than what follows from the above.
Results may differ from the reference program's by a relative error of at most 0.0003.
Values sent between devices are 32-bit elements; how exact they have to be, the bound alone decides.
No kernel may reach another device: no remote copies, remote signals or barrier semaphores. Data moves between devices by JAX's collectives and lax.ppermute only.
A program may use at most 128 MiB of HBM per device.

```python
import math
import jax
import jax.numpy as jnp
from jax import lax

NBLK = 128
NOWN = 2048
GSLOT = 128
REACH = 2
ITERS = 2
NODES = 65536
N_DOM = 8
N_SUB = 4


def ghost_counts(key):
    slot_count = 2 * REACH + 1
    counts = jax.random.randint(jax.random.fold_in(key, 11), (N_DOM, N_SUB, slot_count, N_SUB), GSLOT // 8, GSLOT + 1)
    k = jnp.arange(slot_count)[None, None, :, None]
    s = jnp.arange(N_SUB)[None, :, None, None]
    t = jnp.arange(N_SUB)[None, None, None, :]
    counts = jnp.where((k == slot_count - 1) & (t == N_SUB - 1), GSLOT, counts)
    counts = jnp.where((k == REACH) & (t == s), 0, counts)
    return counts.astype(jnp.int32)


def draw_send_count(key, part):
    return ghost_counts(key)


def draw_send_list(key, part):
    slot_count = 2 * REACH + 1
    lists = jax.random.randint(jax.random.fold_in(key, 12), (N_DOM, N_SUB, slot_count, N_SUB, GSLOT), 0, NOWN)
    lists = lists.at[:, :, 0, 0, 0].set(0)
    lists = lists.at[:, :, 0, 0, 1].set(NOWN - 1)
    return lists.astype(jnp.int32)


def draw_block_nodes(key, part):
    counts = ghost_counts(key)
    slot_count = 2 * REACH + 1
    block_total = NBLK * N_DOM * N_SUB
    grid = (64, block_total)
    part_id = jnp.arange(block_total) // NBLK
    d = (part_id // N_SUB)[None, :]
    s = (part_id % N_SUB)[None, :]
    is_ghost = jax.random.randint(jax.random.fold_in(key, 21), grid, 0, 3) == 0
    k = jax.random.randint(jax.random.fold_in(key, 22), grid, 0, slot_count)
    t = jax.random.randint(jax.random.fold_in(key, 23), grid, 0, N_SUB)
    src_dom = (d - k + REACH) % N_DOM
    live = counts[src_dom, t, k, jnp.broadcast_to(s, grid)]
    j = jax.random.randint(jax.random.fold_in(key, 24), grid, 0, 1 << 20) % jnp.maximum(live, 1)
    ghost_col = NOWN + (k * N_SUB + t) * GSLOT + j
    owned_col = jax.random.randint(jax.random.fold_in(key, 25), grid, 0, NOWN)
    columns = jnp.where(is_ghost & (live > 0), ghost_col, owned_col)
    top_col = NOWN + slot_count * N_SUB * GSLOT - 1
    first_block = jnp.arange(block_total) % NBLK == 0
    forced = first_block & (part_id % N_SUB == N_SUB - 1)
    columns = columns.at[0].set(jnp.where(forced, top_col, columns[0]))
    columns = columns.at[1].set(jnp.where(first_block, 0, columns[1]))
    return columns.astype(jnp.int32)


def draw_tet_corners(key, part):
    tet_total = NBLK * 128 * N_DOM * N_SUB
    base = jax.random.randint(jax.random.fold_in(key, 31), (1, tet_total), 0, 64)
    jitter = jax.random.randint(jax.random.fold_in(key, 32), (4, tet_total), 0, 16)
    lanes = jnp.arange(4)[:, None] * 16
    corners = (base + lanes + jitter) % 64
    corners = corners.at[:, 0].set(jnp.array([0, 21, 42, 63]))
    return corners.astype(jnp.int32)


def touch_ends(entries, stream_key, low, largest):
    longest = entries.shape.index(max(entries.shape))
    spots = []
    for shift in (0, 1):
        where = [jax.random.randint(jax.random.fold_in(stream_key, axis), (), 0, length) for axis, length in enumerate(entries.shape)]
        where[longest] = (where[longest] + shift) % entries.shape[longest]
        spots.append(tuple(where))
    return entries.at[spots[0]].set(low).at[spots[1]].set(largest)


def level_of(rng, extent, split, least, top_value):
    factor_of = 1.0
    for axis_at, shards_of in split:
        draws = jax.random.uniform(jax.random.fold_in(jax.random.fold_in(rng, 6), axis_at), (shards_of,), jnp.float32, least / len(split), top_value / len(split))
        factor_of = factor_of * jnp.repeat(jnp.exp(draws), extent[axis_at] // shards_of).reshape((-1,) + (1,) * (len(extent) - 1 - axis_at))
    return factor_of


def scatter_about(stream_key, extent, deviation, reach, cuts=(), kind=jnp.bfloat16):
    entries = jax.random.normal(stream_key, extent, jnp.float32) * deviation
    if len(cuts) > 0:
        entries = level_of(stream_key, extent, cuts, -0.22, 0.18) * entries
    return jnp.clip(entries, min=-reach, max=reach).astype(kind)


def setup_inputs(seed: int = 0) -> dict:
    seeds = jax.random.split(jax.random.key(seed), 7)
    positions = scatter_about(seeds[0], (3, NODES), 1.0, 6.0, ((1, 32),), jnp.float32)
    fixed_mask = touch_ends((jax.random.randint(seeds[1], (NODES,), 0, 8) < 1).astype(jnp.int32), jax.random.fold_in(seeds[1], 1), 0, 1)
    send_count = draw_send_count(jax.random.fold_in(seeds[6], 71), 0)
    send_list = draw_send_list(jax.random.fold_in(seeds[6], 71), 0)
    block_nodes = draw_block_nodes(jax.random.fold_in(seeds[6], 71), 0)
    tet_corners = draw_tet_corners(jax.random.fold_in(seeds[6], 71), 0)
    return {"positions": positions, "fixed_mask": fixed_mask, "send_count": send_count, "send_list": send_list, "block_nodes": block_nodes, "tet_corners": tet_corners}


delta_reg = 2.0
step_size = 0.01
winv_rows = ((1.0, -1.0 / math.sqrt(3.0), -1.0 / math.sqrt(6.0)), (0.0, 2.0 / math.sqrt(3.0), -1.0 / math.sqrt(6.0)), (0.0, 0.0, math.sqrt(1.5)))

def tet_energy(local_nodes, block_nodes, tet_corners):
    block_total = block_nodes.shape[1]
    tet_total = tet_corners.shape[1]
    owner_block = jnp.arange(tet_total, dtype=jnp.int32) // 128
    flat_nodes = block_nodes.reshape(-1)
    node_ids = flat_nodes[tet_corners * block_total + owner_block[None, :]]
    corners = local_nodes[:, node_ids]
    edge_rows = [[corners[r, m + 1] - corners[r, 0] for m in range(3)] for r in range(3)]
    shape_mat = []
    for r in range(3):
        row_vals = []
        for c in range(3):
            acc_val = None
            for m in range(3):
                if winv_rows[m][c] != 0.0:
                    term_val = edge_rows[r][m] * winv_rows[m][c]
                    acc_val = term_val if acc_val is None else acc_val + term_val
            row_vals.append(acc_val)
        shape_mat.append(row_vals)
    norm_sq = shape_mat[0][0] * shape_mat[0][0]
    for r in range(3):
        for c in range(3):
            if r + c > 0:
                norm_sq = norm_sq + shape_mat[r][c] * shape_mat[r][c]
    volume_det = shape_mat[0][0] * (shape_mat[1][1] * shape_mat[2][2] - shape_mat[1][2] * shape_mat[2][1]) - shape_mat[0][1] * (shape_mat[1][0] * shape_mat[2][2] - shape_mat[1][2] * shape_mat[2][0]) + shape_mat[0][2] * (shape_mat[1][0] * shape_mat[2][1] - shape_mat[1][1] * shape_mat[2][0])
    root_term = jnp.sqrt(volume_det * volume_det + 4.0 * delta_reg * delta_reg)
    upper_part = 0.5 * (volume_det + root_term)
    lower_den = jnp.where(volume_det < 0, root_term - volume_det, 1.0)
    height = jnp.where(volume_det >= 0, upper_part, 2.0 * delta_reg * delta_reg / lower_den)
    distortion = norm_sq / (3.0 * height ** (2.0 / 3.0))
    return jnp.sum(distortion)

def reference(positions, fixed_mask, send_count, send_list, block_nodes, tet_corners):
    dom_count = N_DOM
    sub_count = N_SUB
    slot_count = 2 * REACH + 1
    part_count = dom_count * sub_count
    d = jnp.arange(dom_count, dtype=jnp.int32)[:, None, None, None, None]
    s = jnp.arange(sub_count, dtype=jnp.int32)[None, :, None, None, None]
    k = jnp.arange(slot_count, dtype=jnp.int32)[None, None, :, None, None]
    t = jnp.arange(sub_count, dtype=jnp.int32)[None, None, None, :, None]
    j = jnp.arange(GSLOT, dtype=jnp.int32)[None, None, None, None, :]
    src_dom = (d - k + REACH) % dom_count
    entry_ids = send_list[src_dom, t, k, s, j]
    live_count = send_count[src_dom, t, k, s]
    ghost_ok = (j < live_count).reshape(part_count, -1)
    ghost_ids = ((src_dom * sub_count + t) * NOWN + entry_ids).astype(jnp.int32).reshape(part_count, -1)
    blocks_all = block_nodes.reshape(64, part_count, NBLK).transpose(1, 0, 2)
    corners_all = tet_corners.reshape(4, part_count, NBLK * 128).transpose(1, 0, 2)
    free_nodes = (fixed_mask == 0).astype(positions.dtype)
    grad_fn = jax.grad(tet_energy)
    current = positions
    for step in range(ITERS):

        def visit_part(grad_total, item):
            part, ids_here, ok_here, blocks, corners = item
            start = part * NOWN
            owned_pos = lax.dynamic_slice_in_dim(current, start, NOWN, 1)
            ghosts = jnp.where(ok_here[None, :], current[:, ids_here], 0.0)
            local_nodes = jnp.concatenate([owned_pos, ghosts], axis=1)
            local_grad = grad_fn(local_nodes, blocks, corners)
            own_part = lax.dynamic_slice_in_dim(grad_total, start, NOWN, 1) + local_grad[:, :NOWN]
            grad_total = lax.dynamic_update_slice_in_dim(grad_total, own_part, start, 1)
            grad_total = grad_total.at[:, ids_here].add(jnp.where(ok_here[None, :], local_grad[:, NOWN:], 0.0))
            return (grad_total, None)
        grad_total, _ = lax.scan(visit_part, jnp.zeros_like(current), (jnp.arange(part_count, dtype=jnp.int32), ghost_ids, ghost_ok, blocks_all, corners_all))
        current = current - step_size * free_nodes[None, :] * grad_total
    return current
```

```python
import functools
import math

import jax
import jax.numpy as jnp
from jax import lax
from jax.experimental import pallas as pl
from jax.experimental.pallas import tpu as pltpu
from jax.sharding import PartitionSpec as P

ITERS = 2
LANES = 128
BLOCK_ROWS = 64

delta_reg = 2.0
step_size = 0.01

LANE_GATHER = lax.GatherDimensionNumbers(
    offset_dims=(),
    collapsed_slice_dims=(1,),
    start_index_map=(1,),
    operand_batching_dims=(0,),
    start_indices_batching_dims=(0,),
)


def lane_gather(table, index):
    return lax.gather(
        table,
        index[:, :, None],
        LANE_GATHER,
        slice_sizes=(1, 1),
        mode=lax.GatherScatterMode.PROMISE_IN_BOUNDS,
    )


def row_iota(rows):
    return lax.broadcasted_iota(jnp.int32, (rows, LANES), 0).astype(jnp.float32).astype(jnp.bfloat16)


def row_equals(ids_row, rows):
    packed = jnp.broadcast_to(ids_row.astype(jnp.float32), (16, LANES)).astype(jnp.bfloat16)
    return jnp.concatenate([packed] * (rows // 16), axis=0) == row_iota(rows)


def one_hot(ids_row, rows):
    mask = row_equals(ids_row, rows)
    return jnp.where(mask, jnp.ones((rows, LANES), jnp.bfloat16), jnp.zeros((rows, LANES), jnp.bfloat16))


def split_two(values):
    upper = values.astype(jnp.bfloat16).astype(jnp.float32)
    return upper, values - upper


def masked_rows(mask, row):
    rows = mask.shape[0]
    packed = jnp.broadcast_to(row, (16, LANES)).astype(jnp.bfloat16)
    tiled = jnp.concatenate([packed] * (rows // 16), axis=0)
    return jnp.where(mask, tiled, jnp.zeros((rows, LANES), jnp.bfloat16))


def contract_lanes(a, b):
    return lax.dot_general(a, b, (((1,), (1,)), ((), ())), preferred_element_type=jnp.float32)


def gather_owned(row_of, owned_rows, index):
    low = index & (LANES - 1)
    high = index >> 7
    out = [jnp.zeros(index.shape, jnp.float32) for _ in range(3)]
    for h in range(owned_rows):
        hit = high == h
        for r in range(3):
            table = jnp.broadcast_to(row_of(r, h), index.shape)
            out[r] = jnp.where(hit, lane_gather(table, low), out[r])
    return out


def distortion_gradient(corners):
    edge = [[corners[r][m + 1] - corners[r][0] for m in range(3)] for r in range(3)]
    half = [0.5 * (edge[r][0] + edge[r][1] + edge[r][2]) for r in range(3)]
    bent = [[2.0 * edge[r][m] - half[r] for m in range(3)] for r in range(3)]
    norm_sq = None
    for r in range(3):
        for m in range(3):
            term = edge[r][m] * bent[r][m]
            norm_sq = term if norm_sq is None else norm_sq + term
    cof = [[None] * 3 for _ in range(3)]
    for r in range(3):
        r1, r2 = (r + 1) % 3, (r + 2) % 3
        for m in range(3):
            m1, m2 = (m + 1) % 3, (m + 2) % 3
            cof[r][m] = edge[r1][m1] * edge[r2][m2] - edge[r1][m2] * edge[r2][m1]
    root2 = math.sqrt(2.0)
    volume_det = root2 * (edge[0][0] * cof[0][0] + edge[0][1] * cof[0][1] + edge[0][2] * cof[0][2])
    root_term = jnp.sqrt(volume_det * volume_det + 4.0 * delta_reg * delta_reg)
    spread = root_term + jnp.abs(volume_det)
    height = jnp.where(volume_det >= 0, 0.5 * spread, 2.0 * delta_reg * delta_reg / spread)
    outer = (2.0 / 3.0) * jnp.exp((-2.0 / 3.0) * jnp.log(height))
    inner = norm_sq * (root2 / 3.0) / root_term
    gradient = [[None] * 4 for _ in range(3)]
    for r in range(3):
        for m in range(3):
            gradient[r][m + 1] = outer * (bent[r][m] - inner * cof[r][m])
        gradient[r][0] = -(gradient[r][1] + gradient[r][2] + gradient[r][3])
    return gradient


def write_payload(positions_row, owned_rows, send_list_ref, count_ref, out_ref, dom_count):
    dom_here = lax.axis_index("dom")
    slot_count, sub_count, width = send_list_ref.shape
    reach = (slot_count - 1) // 2
    out_ref[...] = jnp.zeros(out_ref.shape, jnp.float32)
    lane = lax.broadcasted_iota(jnp.int32, (1, LANES), 1)
    for k in range(slot_count):
        picked = gather_owned(positions_row, owned_rows, send_list_ref[k])
        target = lax.rem(dom_here + k - reach + dom_count, dom_count) * sub_count
        for t in range(sub_count):
            valid = lane < count_ref[k, t]
            for r in range(3):
                row = jnp.where(valid, picked[r][t : t + 1, :], 0.0)
                out_ref[pl.ds(target + t, 1), 0, r * LANES : (r + 1) * LANES] = row


def send_kernel(positions_ref, send_list_ref, count_ref, out_ref, *, dom_count):
    owned_rows = positions_ref.shape[1] // LANES
    write_payload(
        lambda r, h: positions_ref[r : r + 1, h * LANES : (h + 1) * LANES],
        owned_rows,
        send_list_ref,
        count_ref,
        out_ref,
        dom_count,
    )


def gradient_kernel(
    positions_ref, ghost_ref, pair_nodes_ref, corner_ref, own_ref, back_ref, terms_ref, total_ref, *, dom_count, slot_count
):
    dom_here = lax.axis_index("dom")
    owned_rows = positions_ref.shape[1] // LANES
    sub_count = ghost_ref.shape[0] // dom_count
    reach = (slot_count - 1) // 2
    pair_count = pair_nodes_ref.shape[0]
    high_rows = owned_rows + slot_count * sub_count
    padded = -(-high_rows // 16) * 16

    def ghost_place(k):
        return lax.rem(dom_here - k + reach + dom_count, dom_count) * sub_count

    def local_row(r, h):
        if h < owned_rows:
            return positions_ref[r : r + 1, h * LANES : (h + 1) * LANES]
        k, t = divmod(h - owned_rows, sub_count)
        return ghost_ref[pl.ds(ghost_place(k) + t, 1), 0, r * LANES : (r + 1) * LANES]

    def tets_of_pairs(g, carry):
        index = pair_nodes_ref[pl.ds(pl.multiple_of(g * 8, 8), 8), :]
        nodes = gather_owned(local_row, high_rows, index)
        for q in range(2):
            corners = [[None] * 4 for _ in range(3)]
            for n in range(4):
                place = corner_ref[n, pl.ds(g * 16 + q, 8, stride=2), :] + q * BLOCK_ROWS
                for r in range(3):
                    corners[r][n] = lane_gather(nodes[r], place)
            gradient = distortion_gradient(corners)
            for r in range(3):
                for n in range(4):
                    terms_ref[n, pl.ds(g * 128 + q * 8 + r, 8, stride=16), :] = gradient[r][n]
        return carry

    lax.fori_loop(0, pair_count // 8, tets_of_pairs, 0)
    total_ref[...] = jnp.zeros(total_ref.shape, jnp.float32)
    first_half = lax.broadcasted_iota(jnp.int32, (8, LANES), 1) < BLOCK_ROWS

    def add_pair(p):
        hits = []
        for n in range(4):
            halves = [one_hot(corner_ref[n, pl.ds(2 * p + q, 1), :], BLOCK_ROWS) for q in range(2)]
            hits.append(jnp.concatenate(halves, axis=0))
        start = pl.multiple_of(p * 16, 16)
        terms = []
        for n in range(4):
            terms.append(jnp.concatenate(split_two(terms_ref[n, pl.ds(start, 16), :]), axis=0).astype(jnp.bfloat16))
        terms = jnp.concatenate(terms, axis=1)
        sums = contract_lanes(terms, jnp.concatenate(hits, axis=1))
        sums = sums[:16] + sums[16:]
        node_sums = jnp.where(first_half, sums[:8], sums[8:])
        index = pair_nodes_ref[pl.ds(p, 1), :]
        mask = row_equals(index >> 7, padded)
        rows = []
        for part in split_two(node_sums):
            for r in range(3):
                rows.append(masked_rows(mask, part[r : r + 1, :]))
        return jnp.concatenate(rows, axis=0), one_hot(index & (LANES - 1), LANES)

    def add_pairs(i, carry):
        left, right = zip(*[add_pair(2 * i + j) for j in range(2)])
        total_ref[...] += contract_lanes(jnp.concatenate(left, axis=1), jnp.concatenate(right, axis=1))
        return carry

    lax.fori_loop(0, pair_count // 2, add_pairs, 0)
    back_ref[...] = jnp.zeros(back_ref.shape, jnp.float32)
    for r in range(3):
        summed = total_ref[r * padded : (r + 1) * padded, :] + total_ref[(3 + r) * padded : (4 + r) * padded, :]
        own_ref[r] = summed[:owned_rows]
        for k in range(slot_count):
            target = ghost_place(k)
            for t in range(sub_count):
                h = owned_rows + k * sub_count + t
                back_ref[pl.ds(target + t, 1), 0, r * LANES : (r + 1) * LANES] = summed[h : h + 1]


def moved_positions(positions_ref, mask_ref, own_ref, back_ref, send_list_ref, count_ref, dom_count):
    dom_here = lax.axis_index("dom")
    slot_count, sub_count, width = send_list_ref.shape
    reach = (slot_count - 1) // 2
    owned_rows = own_ref.shape[1]
    lane = lax.broadcasted_iota(jnp.int32, (1, LANES), 1)
    left, right = [], []
    for k in range(slot_count):
        source = lax.rem(dom_here + k - reach + dom_count, dom_count) * sub_count
        for t in range(sub_count):
            index = send_list_ref[k, t : t + 1, :]
            mask = row_equals(index >> 7, owned_rows)
            valid = lane < count_ref[k, t]
            parts = []
            for r in range(3):
                row = back_ref[pl.ds(source + t, 1), 0, r * LANES : (r + 1) * LANES]
                parts.append(split_two(jnp.where(valid, row, 0.0)))
            left.append(jnp.concatenate([masked_rows(mask, parts[r][s]) for s in range(2) for r in range(3)], axis=0))
            right.append(one_hot(index & (LANES - 1), LANES))
    returned = contract_lanes(jnp.concatenate(left, axis=1), jnp.concatenate(right, axis=1))
    free = jnp.where(mask_ref[...] == 0, step_size, 0.0)
    moved = []
    for r in range(3):
        added = returned[r * owned_rows : (r + 1) * owned_rows] + returned[(3 + r) * owned_rows : (4 + r) * owned_rows]
        here = jnp.concatenate(
            [positions_ref[r : r + 1, h * LANES : (h + 1) * LANES] for h in range(owned_rows)], axis=0
        )
        moved.append(here - free * (own_ref[r] + added))
    return moved


def move_kernel(positions_ref, mask_ref, own_ref, back_ref, send_list_ref, count_ref, *out_refs, dom_count):
    moved = moved_positions(positions_ref, mask_ref, own_ref, back_ref, send_list_ref, count_ref, dom_count)
    owned_rows = own_ref.shape[1]
    for r in range(3):
        for h in range(owned_rows):
            out_refs[0][r : r + 1, h * LANES : (h + 1) * LANES] = moved[r][h : h + 1]
    if len(out_refs) > 1:
        write_payload(
            lambda r, h: moved[r][h : h + 1], owned_rows, send_list_ref, count_ref, out_refs[1], dom_count
        )


def per_device(positions, fixed_mask, send_count, send_list, block_nodes, tet_corners):
    node_count = positions.shape[1]
    slot_count, sub_count, width = send_list.shape[2:]
    dom_count = lax.axis_size("dom")
    block_count = block_nodes.shape[1]
    owned_rows = node_count // LANES
    counts = send_count[0, 0]
    lists = send_list[0, 0]
    mask_rows = fixed_mask.reshape(owned_rows, LANES)
    pair_nodes = block_nodes.T.reshape(block_count // 2, LANES)
    corners = tet_corners.reshape(4, block_count, LANES)
    padded = -(-(owned_rows + slot_count * sub_count) // 16) * 16

    vmem = pl.BlockSpec(memory_space=pltpu.VMEM)
    smem = pl.BlockSpec(memory_space=pltpu.SMEM)
    exchange_shape = jax.ShapeDtypeStruct((dom_count * sub_count, 1, 3 * LANES), jnp.float32)
    position_shape = jax.ShapeDtypeStruct(positions.shape, jnp.float32)
    own_shape = jax.ShapeDtypeStruct((3, owned_rows, LANES), jnp.float32)
    params = pltpu.CompilerParams(vmem_limit_bytes=32 * 1024 * 1024)

    send = pl.pallas_call(
        functools.partial(send_kernel, dom_count=dom_count),
        out_shape=exchange_shape,
        in_specs=[vmem, vmem, smem],
        out_specs=vmem,
        compiler_params=params,
        name="send",
    )
    gradient = pl.pallas_call(
        functools.partial(gradient_kernel, dom_count=dom_count, slot_count=slot_count),
        out_shape=(own_shape, exchange_shape),
        in_specs=[vmem] * 4,
        out_specs=(vmem, vmem),
        scratch_shapes=[
            pltpu.VMEM((4, block_count * 8, LANES), jnp.float32),
            pltpu.VMEM((6 * padded, LANES), jnp.float32),
        ],
        compiler_params=params,
        name="gradient",
    )

    def move(last):
        return pl.pallas_call(
            functools.partial(move_kernel, dom_count=dom_count),
            out_shape=(position_shape,) if last else (position_shape, exchange_shape),
            in_specs=[vmem] * 5 + [smem],
            out_specs=(vmem,) if last else (vmem, vmem),
            compiler_params=params,
            name="move_last" if last else "move",
        )

    def exchange(rows):
        return lax.all_to_all(rows, ("dom", "sub"), 0, 0, tiled=True)

    payload = send(positions, lists, counts)
    for step in range(ITERS):
        last = step == ITERS - 1
        ghosts = exchange(payload)
        own, back = gradient(positions, ghosts, pair_nodes, corners)
        returned = exchange(back)
        moved = move(last)(positions, mask_rows, own, returned, lists, counts)
        positions = moved[0]
        if not last:
            payload = moved[1]
    return positions


def solution(mesh):
    return jax.shard_map(
        per_device,
        mesh=mesh,
        in_specs=(
            P(None, ("dom", "sub")),
            P(("dom", "sub")),
            P("dom", "sub", None, None),
            P("dom", "sub", None, None, None),
            P(None, ("dom", "sub")),
            P(None, ("dom", "sub")),
        ),
        out_specs=P(None, ("dom", "sub")),
        check_vma=False,
    )
```

```python
import functools
import math

import jax
import jax.numpy as jnp
from jax import lax
from jax.experimental import pallas as pl
from jax.experimental.pallas import tpu as pltpu
from jax.sharding import PartitionSpec as P

ITERS = 2
LANES = 128
BLOCK_ROWS = 64

delta_reg = 2.0
step_size = 0.01

LANE_GATHER = lax.GatherDimensionNumbers(
    offset_dims=(),
    collapsed_slice_dims=(1,),
    start_index_map=(1,),
    operand_batching_dims=(0,),
    start_indices_batching_dims=(0,),
)


def lane_gather(table, index):
    return lax.gather(
        table,
        index[:, :, None],
        LANE_GATHER,
        slice_sizes=(1, 1),
        mode=lax.GatherScatterMode.PROMISE_IN_BOUNDS,
    )


def row_iota(rows):
    return lax.broadcasted_iota(jnp.int32, (rows, LANES), 0).astype(jnp.float32).astype(jnp.bfloat16)


def row_equals(ids_row, rows):
    packed = jnp.broadcast_to(ids_row, (16, LANES)).astype(jnp.bfloat16)
    return jnp.concatenate([packed] * (rows // 16), axis=0) == row_iota(rows)


def one_hot(ids_row, rows):
    mask = row_equals(ids_row, rows)
    return jnp.where(mask, jnp.ones((rows, LANES), jnp.bfloat16), jnp.zeros((rows, LANES), jnp.bfloat16))


def split_two(values):
    upper = values.astype(jnp.bfloat16).astype(jnp.float32)
    return upper, values - upper


def masked_rows(mask, row):
    rows = mask.shape[0]
    packed = jnp.broadcast_to(row, (16, LANES)).astype(jnp.bfloat16)
    tiled = jnp.concatenate([packed] * (rows // 16), axis=0)
    return jnp.where(mask, tiled, jnp.zeros((rows, LANES), jnp.bfloat16))


def contract_lanes(a, b):
    return lax.dot_general(a, b, (((1,), (1,)), ((), ())), preferred_element_type=jnp.float32)


def gather_owned(row_of, owned_rows, index):
    low = index & (LANES - 1)
    high = index >> 7
    out = [jnp.zeros(index.shape, jnp.float32) for _ in range(3)]
    for h in range(owned_rows):
        hit = high == h
        for r in range(3):
            table = jnp.broadcast_to(row_of(r, h), index.shape)
            out[r] = jnp.where(hit, lane_gather(table, low), out[r])
    return out


def distortion_gradient(corners):
    edge = [[corners[r][m + 1] - corners[r][0] for m in range(3)] for r in range(3)]
    half = [0.5 * (edge[r][0] + edge[r][1] + edge[r][2]) for r in range(3)]
    bent = [[2.0 * edge[r][m] - half[r] for m in range(3)] for r in range(3)]
    norm_sq = None
    for r in range(3):
        for m in range(3):
            term = edge[r][m] * bent[r][m]
            norm_sq = term if norm_sq is None else norm_sq + term
    cof = [[None] * 3 for _ in range(3)]
    for r in range(3):
        r1, r2 = (r + 1) % 3, (r + 2) % 3
        for m in range(3):
            m1, m2 = (m + 1) % 3, (m + 2) % 3
            cof[r][m] = edge[r1][m1] * edge[r2][m2] - edge[r1][m2] * edge[r2][m1]
    root2 = math.sqrt(2.0)
    volume_det = root2 * (edge[0][0] * cof[0][0] + edge[0][1] * cof[0][1] + edge[0][2] * cof[0][2])
    root_term = jnp.sqrt(volume_det * volume_det + 4.0 * delta_reg * delta_reg)
    spread = root_term + jnp.abs(volume_det)
    height = jnp.where(volume_det >= 0, 0.5 * spread, 2.0 * delta_reg * delta_reg / spread)
    outer = (2.0 / 3.0) * jnp.exp((-2.0 / 3.0) * jnp.log(height))
    inner = norm_sq * (root2 / 3.0) / root_term
    gradient = [[None] * 4 for _ in range(3)]
    for r in range(3):
        for m in range(3):
            gradient[r][m + 1] = outer * (bent[r][m] - inner * cof[r][m])
        gradient[r][0] = -(gradient[r][1] + gradient[r][2] + gradient[r][3])
    return gradient


def write_payload(positions_row, owned_rows, send_list_ref, count_ref, out_ref, dom_count):
    dom_here = lax.axis_index("dom")
    slot_count, sub_count, width = send_list_ref.shape
    reach = (slot_count - 1) // 2
    out_ref[...] = jnp.zeros(out_ref.shape, jnp.float32)
    lane = lax.broadcasted_iota(jnp.int32, (1, LANES), 1)
    for k in range(slot_count):
        picked = gather_owned(positions_row, owned_rows, send_list_ref[k])
        target = lax.rem(dom_here + k - reach + dom_count, dom_count) * sub_count
        for t in range(sub_count):
            valid = lane < count_ref[k, t]
            for r in range(3):
                row = jnp.where(valid, picked[r][t : t + 1, :], 0.0)
                out_ref[pl.ds(target + t, 1), 0, r * LANES : (r + 1) * LANES] = row


def send_kernel(positions_ref, send_list_ref, count_ref, out_ref, *, dom_count):
    owned_rows = positions_ref.shape[1] // LANES
    write_payload(
        lambda r, h: positions_ref[r : r + 1, h * LANES : (h + 1) * LANES],
        owned_rows,
        send_list_ref,
        count_ref,
        out_ref,
        dom_count,
    )


def gradient_kernel(
    positions_ref, ghost_ref, pair_nodes_ref, corner_ref, own_ref, back_ref, place_ref, terms_ref, node_ref, total_ref, *, dom_count, slot_count
):
    dom_here = lax.axis_index("dom")
    owned_rows = positions_ref.shape[1] // LANES
    sub_count = ghost_ref.shape[0] // dom_count
    reach = (slot_count - 1) // 2
    pair_count = pair_nodes_ref.shape[0]
    high_rows = owned_rows + slot_count * sub_count
    padded = -(-high_rows // 16) * 16

    def ghost_place(k):
        return lax.rem(dom_here - k + reach + dom_count, dom_count) * sub_count

    def local_row(r, h):
        if h < owned_rows:
            return positions_ref[r : r + 1, h * LANES : (h + 1) * LANES]
        k, t = divmod(h - owned_rows, sub_count)
        return ghost_ref[pl.ds(ghost_place(k) + t, 1), 0, r * LANES : (r + 1) * LANES]

    def tets_of_pairs(g):
        index = pair_nodes_ref[pl.ds(g * 8, 8), :]
        nodes = gather_owned(local_row, high_rows, index)
        for q in range(2):
            corners = [[None] * 4 for _ in range(3)]
            for n in range(4):
                place = corner_ref[n, pl.ds(g * 16 + q, 8, stride=2), :]
                place_ref[n, pl.ds(g * 16 + q, 8, stride=2), :] = place.astype(jnp.float32)
                place = place + q * BLOCK_ROWS
                for r in range(3):
                    corners[r][n] = lane_gather(nodes[r], place)
            gradient = distortion_gradient(corners)
            for r in range(3):
                for n in range(4):
                    for s, part in enumerate(split_two(gradient[r][n])):
                        terms_ref[n, pl.ds(g * 128 + q * 8 + s * 4 + r, 8, stride=16), :] = part

    for g in range(pair_count // 8):
        tets_of_pairs(g)
    first_half = lax.broadcasted_iota(jnp.int32, (8, LANES), 1) < BLOCK_ROWS

    def add_tets(p):
        hits = []
        for n in range(4):
            halves = [one_hot(place_ref[n, pl.ds(2 * p + q, 1), :], BLOCK_ROWS) for q in range(2)]
            hits.append(jnp.concatenate(halves, axis=0))
        terms = [terms_ref[n, pl.ds(p * 16, 16), :].astype(jnp.bfloat16) for n in range(4)]
        sums = contract_lanes(jnp.concatenate(terms, axis=1), jnp.concatenate(hits, axis=1))
        sums = jnp.where(first_half, sums[:8], sums[8:])
        node_ref[pl.ds(p * 8, 8), :] = sums + pltpu.roll(sums, 4, 0)

    for p in range(pair_count):
        add_tets(p)

    def node_rows(p):
        index = pair_nodes_ref[pl.ds(p, 1), :]
        mask = row_equals((index >> 7).astype(jnp.float32), padded)
        rows = []
        for part in split_two(node_ref[pl.ds(p * 8, 8), :]):
            for r in range(3):
                rows.append(masked_rows(mask, part[r : r + 1, :]))
        return jnp.concatenate(rows, axis=0), one_hot((index & (LANES - 1)).astype(jnp.float32), LANES)

    left, right = zip(*[node_rows(p) for p in range(pair_count)])
    total_ref[...] = contract_lanes(jnp.concatenate(left, axis=1), jnp.concatenate(right, axis=1))
    back_ref[...] = jnp.zeros(back_ref.shape, jnp.float32)
    for r in range(3):
        summed = total_ref[r * padded : (r + 1) * padded, :] + total_ref[(3 + r) * padded : (4 + r) * padded, :]
        own_ref[r] = summed[:owned_rows]
        for k in range(slot_count):
            target = ghost_place(k)
            for t in range(sub_count):
                h = owned_rows + k * sub_count + t
                back_ref[pl.ds(target + t, 1), 0, r * LANES : (r + 1) * LANES] = summed[h : h + 1]


def moved_positions(positions_ref, mask_ref, own_ref, back_ref, send_list_ref, count_ref, dom_count):
    dom_here = lax.axis_index("dom")
    slot_count, sub_count, width = send_list_ref.shape
    reach = (slot_count - 1) // 2
    owned_rows = own_ref.shape[1]
    lane = lax.broadcasted_iota(jnp.int32, (1, LANES), 1)
    left, right = [], []
    for k in range(slot_count):
        source = lax.rem(dom_here + k - reach + dom_count, dom_count) * sub_count
        for t in range(sub_count):
            index = send_list_ref[k, t : t + 1, :]
            mask = row_equals((index >> 7).astype(jnp.float32), owned_rows)
            valid = lane < count_ref[k, t]
            parts = []
            for r in range(3):
                row = back_ref[pl.ds(source + t, 1), 0, r * LANES : (r + 1) * LANES]
                parts.append(split_two(jnp.where(valid, row, 0.0)))
            left.append(jnp.concatenate([masked_rows(mask, parts[r][s]) for s in range(2) for r in range(3)], axis=0))
            right.append(one_hot((index & (LANES - 1)).astype(jnp.float32), LANES))
    returned = contract_lanes(jnp.concatenate(left, axis=1), jnp.concatenate(right, axis=1))
    free = jnp.where(mask_ref[...] == 0, step_size, 0.0)
    moved = []
    for r in range(3):
        added = returned[r * owned_rows : (r + 1) * owned_rows] + returned[(3 + r) * owned_rows : (4 + r) * owned_rows]
        here = jnp.concatenate(
            [positions_ref[r : r + 1, h * LANES : (h + 1) * LANES] for h in range(owned_rows)], axis=0
        )
        moved.append(here - free * (own_ref[r] + added))
    return moved


def move_kernel(positions_ref, mask_ref, own_ref, back_ref, send_list_ref, count_ref, *out_refs, dom_count):
    moved = moved_positions(positions_ref, mask_ref, own_ref, back_ref, send_list_ref, count_ref, dom_count)
    owned_rows = own_ref.shape[1]
    for r in range(3):
        for h in range(owned_rows):
            out_refs[0][r : r + 1, h * LANES : (h + 1) * LANES] = moved[r][h : h + 1]
    if len(out_refs) > 1:
        write_payload(
            lambda r, h: moved[r][h : h + 1], owned_rows, send_list_ref, count_ref, out_refs[1], dom_count
        )


def per_device(positions, fixed_mask, send_count, send_list, block_nodes, tet_corners):
    node_count = positions.shape[1]
    slot_count, sub_count, width = send_list.shape[2:]
    dom_count = lax.axis_size("dom")
    block_count = block_nodes.shape[1]
    owned_rows = node_count // LANES
    counts = send_count[0, 0]
    lists = send_list[0, 0]
    mask_rows = fixed_mask.reshape(owned_rows, LANES)
    pair_nodes = block_nodes.T.reshape(block_count // 2, LANES)
    corners = tet_corners.reshape(4, block_count, LANES)
    padded = -(-(owned_rows + slot_count * sub_count) // 16) * 16

    vmem = pl.BlockSpec(memory_space=pltpu.VMEM)
    smem = pl.BlockSpec(memory_space=pltpu.SMEM)
    exchange_shape = jax.ShapeDtypeStruct((dom_count * sub_count, 1, 3 * LANES), jnp.float32)
    position_shape = jax.ShapeDtypeStruct(positions.shape, jnp.float32)
    own_shape = jax.ShapeDtypeStruct((3, owned_rows, LANES), jnp.float32)
    params = pltpu.CompilerParams(vmem_limit_bytes=32 * 1024 * 1024)

    send = pl.pallas_call(
        functools.partial(send_kernel, dom_count=dom_count),
        out_shape=exchange_shape,
        in_specs=[vmem, vmem, smem],
        out_specs=vmem,
        compiler_params=params,
        name="send",
    )
    gradient = pl.pallas_call(
        functools.partial(gradient_kernel, dom_count=dom_count, slot_count=slot_count),
        out_shape=(own_shape, exchange_shape),
        in_specs=[vmem] * 4,
        out_specs=(vmem, vmem),
        scratch_shapes=[
            pltpu.VMEM((4, block_count, LANES), jnp.float32),
            pltpu.VMEM((4, block_count * 8, LANES), jnp.float32),
            pltpu.VMEM((block_count * 4, LANES), jnp.float32),
            pltpu.VMEM((6 * padded, LANES), jnp.float32),
        ],
        compiler_params=params,
        name="gradient",
    )

    def move(last):
        return pl.pallas_call(
            functools.partial(move_kernel, dom_count=dom_count),
            out_shape=(position_shape,) if last else (position_shape, exchange_shape),
            in_specs=[vmem] * 5 + [smem],
            out_specs=(vmem,) if last else (vmem, vmem),
            compiler_params=params,
            name="move_last" if last else "move",
        )

    def exchange(rows):
        return lax.all_to_all(rows, ("dom", "sub"), 0, 0, tiled=True)

    payload = send(positions, lists, counts)
    for step in range(ITERS):
        last = step == ITERS - 1
        ghosts = exchange(payload)
        own, back = gradient(positions, ghosts, pair_nodes, corners)
        returned = exchange(back)
        moved = move(last)(positions, mask_rows, own, returned, lists, counts)
        positions = moved[0]
        if not last:
            payload = moved[1]
    return positions


def solution(mesh):
    return jax.shard_map(
        per_device,
        mesh=mesh,
        in_specs=(
            P(None, ("dom", "sub")),
            P(("dom", "sub")),
            P("dom", "sub", None, None),
            P("dom", "sub", None, None, None),
            P(None, ("dom", "sub")),
            P(None, ("dom", "sub")),
        ),
        out_specs=P(None, ("dom", "sub")),
        check_vma=False,
    )
```

```python
import functools
import math

import jax
import jax.numpy as jnp
from jax import lax
from jax.experimental import pallas as pl
from jax.experimental.pallas import tpu as pltpu
from jax.sharding import PartitionSpec as P

ITERS = 2
LANES = 128
BLOCK_ROWS = 64

delta_reg = 2.0
step_size = 0.01

LANE_GATHER = lax.GatherDimensionNumbers(
    offset_dims=(),
    collapsed_slice_dims=(1,),
    start_index_map=(1,),
    operand_batching_dims=(0,),
    start_indices_batching_dims=(0,),
)


def lane_gather(table, index):
    return lax.gather(
        table,
        index[:, :, None],
        LANE_GATHER,
        slice_sizes=(1, 1),
        mode=lax.GatherScatterMode.PROMISE_IN_BOUNDS,
    )


def row_iota(rows):
    return lax.broadcasted_iota(jnp.int32, (rows, LANES), 0).astype(jnp.float32).astype(jnp.bfloat16)


def row_equals(ids_row, rows):
    packed = jnp.broadcast_to(ids_row, (16, LANES)).astype(jnp.bfloat16)
    return jnp.concatenate([packed] * (rows // 16), axis=0) == row_iota(rows)


def one_hot(ids_row, rows):
    mask = row_equals(ids_row, rows)
    return jnp.where(mask, jnp.ones((rows, LANES), jnp.bfloat16), jnp.zeros((rows, LANES), jnp.bfloat16))


def split_two(values):
    upper = values.astype(jnp.bfloat16).astype(jnp.float32)
    return upper, values - upper


def masked_rows(mask, row):
    rows = mask.shape[0]
    packed = jnp.broadcast_to(row, (16, LANES)).astype(jnp.bfloat16)
    tiled = jnp.concatenate([packed] * (rows // 16), axis=0)
    return jnp.where(mask, tiled, jnp.zeros((rows, LANES), jnp.bfloat16))


def contract_lanes(a, b):
    return lax.dot_general(a, b, (((1,), (1,)), ((), ())), preferred_element_type=jnp.float32)


def gather_rows(row_of, first, last, index, out):
    low = index & (LANES - 1)
    high = index >> 7
    out = list(out)
    for h in range(first, last):
        hit = high == h
        for r in range(3):
            table = jnp.broadcast_to(row_of(r, h), index.shape)
            out[r] = jnp.where(hit, lane_gather(table, low), out[r])
    return out


def distortion_gradient(corners):
    edge = [[corners[r][m + 1] - corners[r][0] for m in range(3)] for r in range(3)]
    half = [0.5 * (edge[r][0] + edge[r][1] + edge[r][2]) for r in range(3)]
    bent = [[2.0 * edge[r][m] - half[r] for m in range(3)] for r in range(3)]
    norm_sq = None
    for r in range(3):
        for m in range(3):
            term = edge[r][m] * bent[r][m]
            norm_sq = term if norm_sq is None else norm_sq + term
    cof = [[None] * 3 for _ in range(3)]
    for r in range(3):
        r1, r2 = (r + 1) % 3, (r + 2) % 3
        for m in range(3):
            m1, m2 = (m + 1) % 3, (m + 2) % 3
            cof[r][m] = edge[r1][m1] * edge[r2][m2] - edge[r1][m2] * edge[r2][m1]
    root2 = math.sqrt(2.0)
    volume_det = root2 * (edge[0][0] * cof[0][0] + edge[0][1] * cof[0][1] + edge[0][2] * cof[0][2])
    root_term = jnp.sqrt(volume_det * volume_det + 4.0 * delta_reg * delta_reg)
    spread = root_term + jnp.abs(volume_det)
    height = jnp.where(volume_det >= 0, 0.5 * spread, 2.0 * delta_reg * delta_reg / spread)
    outer = (2.0 / 3.0) * jnp.exp((-2.0 / 3.0) * jnp.log(height))
    inner = norm_sq * (root2 / 3.0) / root_term
    gradient = [[None] * 4 for _ in range(3)]
    for r in range(3):
        for m in range(3):
            gradient[r][m + 1] = outer * (bent[r][m] - inner * cof[r][m])
        gradient[r][0] = -(gradient[r][1] + gradient[r][2] + gradient[r][3])
    return gradient


def position_row(positions_ref):
    return lambda r, h: positions_ref[r : r + 1, h * LANES : (h + 1) * LANES]


def write_payload(row_of, owned_rows, list_ref, valid_ref, out_ref, dom_count):
    dom_here = lax.axis_index("dom")
    slot_count, sub_count, width = list_ref.shape
    reach = (slot_count - 1) // 2
    out_ref[...] = jnp.zeros(out_ref.shape, jnp.float32)
    group = max(1, 8 // sub_count)
    for first in range(0, slot_count, group):
        slots = range(first, min(first + group, slot_count))
        index = jnp.concatenate([list_ref[k] for k in slots], axis=0)
        valid = jnp.concatenate([valid_ref[k] for k in slots], axis=0)
        zeros = [jnp.zeros(index.shape, jnp.float32)] * 3
        picked = [x * valid for x in gather_rows(row_of, 0, owned_rows, index, zeros)]
        for i, k in enumerate(slots):
            target = lax.rem(dom_here + k - reach + dom_count, dom_count) * sub_count
            for t in range(sub_count):
                for r in range(3):
                    row = picked[r][i * sub_count + t : i * sub_count + t + 1, :]
                    out_ref[pl.ds(target + t, 1), 0, r * LANES : (r + 1) * LANES] = row


def send_kernel(positions_hbm, list_hbm, count_hbm, out_ref, valid_ref, positions_ref, list_ref, count_ref, sems, *, dom_count):
    copies = [
        pltpu.make_async_copy(source, target, sems.at[i])
        for i, (source, target) in enumerate(
            [(positions_hbm, positions_ref), (list_hbm, list_ref), (count_hbm, count_ref)]
        )
    ]
    for copy in copies:
        copy.start()
    for copy in copies:
        copy.wait()
    slot_count, sub_count, width = list_ref.shape
    lane = lax.broadcasted_iota(jnp.int32, (sub_count, LANES), 1)
    for k in range(slot_count):
        counts = jnp.broadcast_to(count_ref[:, k : k + 1], (sub_count, LANES))
        valid_ref[k] = jnp.where(lane < counts, 1.0, 0.0)
    write_payload(
        position_row(positions_ref), positions_ref.shape[1] // LANES, list_ref, valid_ref, out_ref, dom_count
    )


def owned_nodes_kernel(positions_ref, pair_nodes_ref, nodes_ref):
    owned_rows = positions_ref.shape[1] // LANES
    for g in range(pair_nodes_ref.shape[0] // 8):
        index = pair_nodes_ref[g * 8 : (g + 1) * 8, :]
        zeros = [jnp.zeros(index.shape, jnp.float32)] * 3
        found = gather_rows(position_row(positions_ref), 0, owned_rows, index, zeros)
        for r in range(3):
            nodes_ref[r, g * 8 : (g + 1) * 8, :] = found[r]


def spread_rows(high_row, parts, rows):
    tiles, place = [], {}
    full, rest = divmod(rows, 16)
    for i, part in enumerate(parts):
        packed = jnp.broadcast_to(part, (16, LANES)).astype(jnp.bfloat16)
        parts[i] = packed
    high = jnp.broadcast_to(high_row, (16, LANES)).astype(jnp.bfloat16)
    zero = jnp.zeros((16, LANES), jnp.bfloat16)
    row = row_iota(16)
    for f in range(full):
        mask = (high - 16.0 * f) == row
        for i, part in enumerate(parts):
            place.update({(i, 16 * f + h): len(tiles) * 16 + h for h in range(16)})
            tiles.append(jnp.where(mask, part, zero))
    if rest:
        share = 16 // rest
        for first in range(0, len(parts), share):
            tile = zero
            for j, i in enumerate(range(first, min(first + share, len(parts)))):
                place.update({(i, 16 * full + h): len(tiles) * 16 + j * rest + h for h in range(rest)})
                shifted = high - (16.0 * full - j * rest)
                mask = (shifted == row) & (high >= 16.0 * full)
                mask = mask & (high < 16.0 * full + rest)
                tile = jnp.where(mask, parts[i], tile)
            tiles.append(tile)
    return jnp.concatenate(tiles, axis=0), place


def column_sums(node_ref, pair_nodes_ref, rows):
    left, right = [], []
    place = None
    for p in range(pair_nodes_ref.shape[0]):
        index = pair_nodes_ref[p : p + 1, :]
        parts = [part[r : r + 1, :] for part in split_two(node_ref[p * 8 : (p + 1) * 8, :]) for r in range(3)]
        spread, place = spread_rows((index >> 7).astype(jnp.float32), parts, rows)
        left.append(spread)
        right.append(one_hot((index & (LANES - 1)).astype(jnp.float32), LANES))
    total = contract_lanes(jnp.concatenate(left, axis=1), jnp.concatenate(right, axis=1))

    def row(r, h):
        upper, lower = place[r, h], place[3 + r, h]
        return total[upper : upper + 1, :] + total[lower : lower + 1, :]

    return row


def gradient_kernel(
    start_ref, ghost_ref, pair_nodes_ref, corner_ref, own_ref, back_ref, place_ref, terms_ref, node_ref, *, dom_count, slot_count
):
    owned_rows = own_ref.shape[1]
    dom_here = lax.axis_index("dom")
    sub_count = ghost_ref.shape[0] // dom_count
    reach = (slot_count - 1) // 2
    pair_count = pair_nodes_ref.shape[0]
    ghost_rows = slot_count * sub_count

    def ghost_place(k):
        return lax.rem(dom_here - k + reach + dom_count, dom_count) * sub_count

    def ghost_row(r, h):
        k, t = divmod(h - owned_rows, sub_count)
        return ghost_ref[pl.ds(ghost_place(k) + t, 1), 0, r * LANES : (r + 1) * LANES]

    def tets_of_pairs(g):
        index = pair_nodes_ref[g * 8 : (g + 1) * 8, :]
        if len(start_ref.shape) == 3:
            nodes = [start_ref[r, g * 8 : (g + 1) * 8, :] for r in range(3)]
        else:
            nodes = [jnp.zeros(index.shape, jnp.float32)] * 3
            nodes = gather_rows(position_row(start_ref), 0, owned_rows, index, nodes)
        nodes = gather_rows(ghost_row, owned_rows, owned_rows + ghost_rows, index, nodes)
        for q in range(2):
            corners = [[None] * 4 for _ in range(3)]
            for n in range(4):
                place = corner_ref[n, pl.ds(g * 16 + q, 8, stride=2), :]
                place_ref[n, pl.ds(g * 16 + q, 8, stride=2), :] = place.astype(jnp.float32)
                for r in range(3):
                    corners[r][n] = lane_gather(nodes[r], place + q * BLOCK_ROWS)
            gradient = distortion_gradient(corners)
            for r in range(3):
                for m in range(3):
                    for s, part in enumerate(split_two(gradient[r][m + 1])):
                        terms_ref[m * 2 + q, pl.ds(g * 64 + s * 4 + r, 8, stride=8), :] = part

    def add_tets(p):
        empty = jnp.zeros((8, LANES), jnp.float32)
        base = [one_hot(place_ref[0, 2 * p + q : 2 * p + q + 1, :], BLOCK_ROWS) for q in range(2)]
        hits, terms = [], []
        for m in range(3):
            for q in range(2):
                hits.append(one_hot(place_ref[m + 1, 2 * p + q : 2 * p + q + 1, :], BLOCK_ROWS) - base[q])
                part = terms_ref[m * 2 + q, p * 8 : (p + 1) * 8, :]
                part = jnp.concatenate([part, empty] if q == 0 else [empty, part], axis=0)
                terms.append(part.astype(jnp.bfloat16))
        sums = contract_lanes(jnp.concatenate(terms, axis=1), jnp.concatenate(hits, axis=1))
        sums = jnp.concatenate([sums[:8], sums[8:]], axis=1)
        node_ref[p * 8 : (p + 1) * 8, :] = sums + pltpu.roll(sums, 4, 0)

    for g in range(pair_count // 8):
        tets_of_pairs(g)
    for p in range(pair_count):
        add_tets(p)
    back_ref[...] = jnp.zeros(back_ref.shape, jnp.float32)
    row = column_sums(node_ref, pair_nodes_ref, owned_rows + ghost_rows)
    for r in range(3):
        for h in range(owned_rows):
            own_ref[r, h : h + 1, :] = row(r, h)
        for k in range(slot_count):
            for t in range(sub_count):
                place = ghost_place(k) + t
                back_ref[pl.ds(place, 1), 0, r * LANES : (r + 1) * LANES] = row(r, owned_rows + k * sub_count + t)


def moved_positions(positions_ref, mask_ref, own_ref, back_ref, list_ref, valid_ref, dom_count):
    dom_here = lax.axis_index("dom")
    slot_count, sub_count, width = list_ref.shape
    reach = (slot_count - 1) // 2
    owned_rows = own_ref.shape[1]
    left, right = [], []
    for k in range(slot_count):
        source = lax.rem(dom_here + k - reach + dom_count, dom_count) * sub_count
        for t in range(sub_count):
            index = list_ref[k, t : t + 1, :]
            valid = valid_ref[k, t : t + 1, :] > 0.0
            mask = row_equals((index >> 7).astype(jnp.float32), owned_rows)
            parts = []
            for r in range(3):
                row = back_ref[pl.ds(source + t, 1), 0, r * LANES : (r + 1) * LANES]
                parts.append(split_two(jnp.where(valid, row, 0.0)))
            left.append(jnp.concatenate([masked_rows(mask, parts[r][s]) for s in range(2) for r in range(3)], axis=0))
            right.append(one_hot((index & (LANES - 1)).astype(jnp.float32), LANES))
    returned = contract_lanes(jnp.concatenate(left, axis=1), jnp.concatenate(right, axis=1))
    free = jnp.where(mask_ref[...] == 0, step_size, 0.0)
    moved = []
    for r in range(3):
        added = returned[r * owned_rows : (r + 1) * owned_rows] + returned[(3 + r) * owned_rows : (4 + r) * owned_rows]
        here = jnp.concatenate(
            [positions_ref[r : r + 1, h * LANES : (h + 1) * LANES] for h in range(owned_rows)], axis=0
        )
        moved.append(here - free * (own_ref[r] + added))
    return moved


def move_kernel(positions_ref, mask_ref, own_ref, back_ref, list_ref, valid_ref, *out_refs, dom_count):
    moved = moved_positions(positions_ref, mask_ref, own_ref, back_ref, list_ref, valid_ref, dom_count)
    owned_rows = own_ref.shape[1]
    for r in range(3):
        for h in range(owned_rows):
            out_refs[0][r : r + 1, h * LANES : (h + 1) * LANES] = moved[r][h : h + 1]
    if len(out_refs) > 1:
        write_payload(lambda r, h: moved[r][h : h + 1], owned_rows, list_ref, valid_ref, out_refs[1], dom_count)


def per_device(positions, fixed_mask, send_count, send_list, block_nodes, tet_corners):
    node_count = positions.shape[1]
    slot_count, sub_count, width = send_list.shape[2:]
    dom_count = lax.axis_size("dom")
    block_count = block_nodes.shape[1]
    owned_rows = node_count // LANES
    counts = send_count[0, 0].T
    lists = send_list[0, 0]
    mask_rows = fixed_mask.reshape(owned_rows, LANES)
    pair_nodes = block_nodes.T.reshape(block_count // 2, LANES)
    corners = tet_corners.reshape(4, block_count, LANES)

    vmem = pl.BlockSpec(memory_space=pltpu.VMEM)
    hbm = pl.BlockSpec(memory_space=pl.ANY)
    exchange_shape = jax.ShapeDtypeStruct((dom_count * sub_count, 1, 3 * LANES), jnp.float32)
    position_shape = jax.ShapeDtypeStruct(positions.shape, jnp.float32)
    params = pltpu.CompilerParams(vmem_limit_bytes=32 * 1024 * 1024)

    def call(kernel, name, ins, outs, scratch=(), **sizes):
        return pl.pallas_call(
            functools.partial(kernel, **sizes),
            out_shape=outs,
            in_specs=ins,
            out_specs=jax.tree.map(lambda _: vmem, outs),
            scratch_shapes=scratch,
            compiler_params=params,
            name=name,
        )

    send = call(
        send_kernel,
        "send",
        [hbm] * 3,
        (exchange_shape, jax.ShapeDtypeStruct(lists.shape, jnp.float32)),
        [
            pltpu.VMEM(positions.shape, jnp.float32),
            pltpu.VMEM(lists.shape, jnp.int32),
            pltpu.VMEM(counts.shape, jnp.int32),
            pltpu.SemaphoreType.DMA((3,)),
        ],
        dom_count=dom_count,
    )
    owned_nodes = call(
        owned_nodes_kernel, "owned_nodes", [vmem] * 2, jax.ShapeDtypeStruct((3,) + pair_nodes.shape, jnp.float32)
    )
    own_shape = jax.ShapeDtypeStruct((3, owned_rows, LANES), jnp.float32)
    gradient = call(
        gradient_kernel,
        "gradient",
        [vmem] * 4,
        (own_shape, exchange_shape),
        [
            pltpu.VMEM((4, block_count, LANES), jnp.float32),
            pltpu.VMEM((6, block_count * 4, LANES), jnp.float32),
            pltpu.VMEM((block_count * 4, LANES), jnp.float32),
        ],
        dom_count=dom_count,
        slot_count=slot_count,
    )

    def exchange(rows):
        return lax.all_to_all(rows, ("dom", "sub"), 0, 0, tiled=True)

    payload, valid = send(*[pltpu.with_memory_space_constraint(x, pltpu.HBM) for x in (positions, lists, counts)])
    for step in range(ITERS):
        last = step == ITERS - 1
        ghosts = exchange(payload)
        start = owned_nodes(positions, pair_nodes) if step == 0 else positions
        own, back = gradient(start, ghosts, pair_nodes, corners)
        returned = exchange(back)
        move = call(
            move_kernel,
            "move_last" if last else "move",
            [vmem] * 6,
            (position_shape,) if last else (position_shape, exchange_shape),
            dom_count=dom_count,
        )
        moved = move(positions, mask_rows, own, returned, lists, valid)
        positions = moved[0]
        if not last:
            payload = moved[1]
    return positions


def solution(mesh):
    return jax.shard_map(
        per_device,
        mesh=mesh,
        in_specs=(
            P(None, ("dom", "sub")),
            P(("dom", "sub")),
            P("dom", "sub", None, None),
            P("dom", "sub", None, None, None),
            P(None, ("dom", "sub")),
            P(None, ("dom", "sub")),
        ),
        out_specs=P(None, ("dom", "sub")),
        check_vma=False,
    )
```

```python
import functools
import math

import jax
import jax.numpy as jnp
from jax import lax
from jax.experimental import pallas as pl
from jax.experimental.pallas import tpu as pltpu
from jax.sharding import PartitionSpec as P

ITERS = 2
LANES = 128
BLOCK_ROWS = 64

delta_reg = 2.0
step_size = 0.01

LANE_GATHER = lax.GatherDimensionNumbers(
    offset_dims=(),
    collapsed_slice_dims=(1,),
    start_index_map=(1,),
    operand_batching_dims=(0,),
    start_indices_batching_dims=(0,),
)


def lane_gather(table, index):
    return lax.gather(
        table,
        index[:, :, None],
        LANE_GATHER,
        slice_sizes=(1, 1),
        mode=lax.GatherScatterMode.PROMISE_IN_BOUNDS,
    )


def row_iota(rows):
    return lax.broadcasted_iota(jnp.int32, (rows, LANES), 0).astype(jnp.float32).astype(jnp.bfloat16)


def row_equals(ids_row, rows):
    packed = jnp.broadcast_to(ids_row, (16, LANES)).astype(jnp.int16)
    return jnp.concatenate([packed] * (rows // 16), axis=0) == lax.broadcasted_iota(jnp.int32, (rows, LANES), 0).astype(jnp.int16)


def one_hot(ids_row, rows, value=1.0):
    mask = row_equals(ids_row, rows)
    return jnp.where(mask, jnp.full((rows, LANES), value, jnp.bfloat16), jnp.zeros((rows, LANES), jnp.bfloat16))


def split_two(values):
    upper = values.astype(jnp.bfloat16).astype(jnp.float32)
    return upper, values - upper


def masked_rows(mask, row):
    rows = mask.shape[0]
    packed = jnp.broadcast_to(row, (16, LANES)).astype(jnp.bfloat16)
    tiled = jnp.concatenate([packed] * (rows // 16), axis=0)
    return jnp.where(mask, tiled, jnp.zeros((rows, LANES), jnp.bfloat16))


def contract_lanes(a, b):
    return lax.dot_general(a, b, (((1,), (1,)), ((), ())), preferred_element_type=jnp.float32)


def gather_rows(row_of, first, last, index, out):
    low = index & (LANES - 1)
    high = index >> 7
    out = list(out)
    for h in range(first, last):
        hit = high == h
        for r in range(3):
            table = jnp.broadcast_to(row_of(r, h), index.shape)
            out[r] = jnp.where(hit, lane_gather(table, low), out[r])
    return out


def distortion_gradient(corners):
    edge = [[corners[r][m + 1] - corners[r][0] for m in range(3)] for r in range(3)]
    half = [0.5 * (edge[r][0] + edge[r][1] + edge[r][2]) for r in range(3)]
    bent = [[2.0 * edge[r][m] - half[r] for m in range(3)] for r in range(3)]
    norm_sq = None
    for r in range(3):
        for m in range(3):
            term = edge[r][m] * bent[r][m]
            norm_sq = term if norm_sq is None else norm_sq + term
    cof = [[None] * 3 for _ in range(3)]
    for r in range(3):
        r1, r2 = (r + 1) % 3, (r + 2) % 3
        for m in range(3):
            m1, m2 = (m + 1) % 3, (m + 2) % 3
            cof[r][m] = edge[r1][m1] * edge[r2][m2] - edge[r1][m2] * edge[r2][m1]
    root2 = math.sqrt(2.0)
    volume_det = root2 * (edge[0][0] * cof[0][0] + edge[0][1] * cof[0][1] + edge[0][2] * cof[0][2])
    root_term = jnp.sqrt(volume_det * volume_det + 4.0 * delta_reg * delta_reg)
    spread = root_term + jnp.abs(volume_det)
    height = jnp.where(volume_det >= 0, 0.5 * spread, 2.0 * delta_reg * delta_reg / spread)
    outer = (2.0 / 3.0) * jnp.exp((-2.0 / 3.0) * jnp.log(height))
    inner = norm_sq * (root2 / 3.0) / root_term
    gradient = [[None] * 4 for _ in range(3)]
    for r in range(3):
        for m in range(3):
            gradient[r][m + 1] = outer * (bent[r][m] - inner * cof[r][m])
        gradient[r][0] = -(gradient[r][1] + gradient[r][2] + gradient[r][3])
    return gradient


def position_row(positions_ref):
    return lambda r, h: positions_ref[r : r + 1, h * LANES : (h + 1) * LANES]


def write_payload(row_of, owned_rows, list_ref, valid_ref, out_ref, dom_count):
    dom_here = lax.axis_index("dom")
    slot_count, sub_count, width = list_ref.shape
    reach = (slot_count - 1) // 2
    out_ref[...] = jnp.zeros(out_ref.shape, jnp.float32)
    group = max(1, 8 // sub_count)
    for first in range(0, slot_count, group):
        slots = range(first, min(first + group, slot_count))
        index = jnp.concatenate([list_ref[k] for k in slots], axis=0)
        valid = jnp.concatenate([valid_ref[k] for k in slots], axis=0)
        zeros = [jnp.zeros(index.shape, jnp.float32)] * 3
        picked = [x * valid for x in gather_rows(row_of, 0, owned_rows, index, zeros)]
        for i, k in enumerate(slots):
            target = lax.rem(dom_here + k - reach + dom_count, dom_count) * sub_count
            for t in range(sub_count):
                for r in range(3):
                    row = picked[r][i * sub_count + t : i * sub_count + t + 1, :]
                    out_ref[pl.ds(target + t, 1), 0, r * LANES : (r + 1) * LANES] = row


def send_kernel(
    positions_hbm,
    list_hbm,
    count_hbm,
    block_nodes_hbm,
    corner_hbm,
    out_ref,
    valid_ref,
    pair_nodes_ref,
    corner_ref,
    positions_ref,
    list_ref,
    count_ref,
    block_nodes_ref,
    sems,
    *,
    dom_count,
):
    copies = [
        pltpu.make_async_copy(source, target, sems.at[i])
        for i, (source, target) in enumerate(
            [
                (positions_hbm, positions_ref),
                (list_hbm, list_ref),
                (count_hbm, count_ref),
                (block_nodes_hbm, block_nodes_ref),
                (corner_hbm, corner_ref),
            ]
        )
    ]
    for copy in copies:
        copy.start()
    for copy in copies[:3]:
        copy.wait()
    slot_count, sub_count, width = list_ref.shape
    lane = lax.broadcasted_iota(jnp.int32, (sub_count, LANES), 1)
    for k in range(slot_count):
        counts = jnp.broadcast_to(count_ref[:, k : k + 1], (sub_count, LANES))
        valid_ref[k] = jnp.where(lane < counts, 1.0, 0.0)
    write_payload(
        position_row(positions_ref), positions_ref.shape[1] // LANES, list_ref, valid_ref, out_ref, dom_count
    )
    copies[3].wait()
    half = pair_nodes_ref.shape[0]
    nodes = block_nodes_ref[...].T
    pair_nodes_ref[...] = jnp.concatenate([nodes[:half], nodes[half:]], axis=1)
    copies[4].wait()


def spread_rows(high_row, parts, rows):
    tiles, place = [], {}
    full, rest = divmod(rows, 16)
    parts = [jnp.broadcast_to(part, (16, LANES)).astype(jnp.bfloat16) for part in parts]
    high = jnp.broadcast_to(high_row, (16, LANES)).astype(jnp.bfloat16)
    zero = jnp.zeros((16, LANES), jnp.bfloat16)
    row = lax.broadcasted_iota(jnp.int32, (16, LANES), 0)
    for f in range(full):
        mask = high == (row + 16 * f).astype(jnp.float32).astype(jnp.bfloat16)
        for i, part in enumerate(parts):
            place.update({(i, 16 * f + h): len(tiles) * 16 + h for h in range(16)})
            tiles.append(jnp.where(mask, part, zero))
    if rest:
        share = 16 // rest
        masks = []
        for j in range(share):
            wanted = jnp.where((row >= j * rest) & (row < (j + 1) * rest), row - j * rest + 16 * full, -1)
            masks.append(high == wanted.astype(jnp.float32).astype(jnp.bfloat16))
        for first in range(0, len(parts), share):
            tile = zero
            for j, i in enumerate(range(first, min(first + share, len(parts)))):
                place.update({(i, 16 * full + h): len(tiles) * 16 + j * rest + h for h in range(rest)})
                tile = jnp.where(masks[j], parts[i], tile)
            tiles.append(tile)
    return jnp.concatenate(tiles, axis=0), place


def column_sums(node_ref, pair_nodes_ref, rows):
    left, right = [], []
    place = None
    for p in range(pair_nodes_ref.shape[0]):
        index = pair_nodes_ref[p : p + 1, :]
        parts = [part[r : r + 1, :] for part in split_two(node_ref[p * 8 : (p + 1) * 8, :]) for r in range(3)]
        spread, place = spread_rows((index >> 7).astype(jnp.float32), parts, rows)
        left.append(spread)
        right.append(one_hot(index & (LANES - 1), LANES))
    total = contract_lanes(jnp.concatenate(left, axis=1), jnp.concatenate(right, axis=1))

    def row(r, h):
        upper, lower = place[r, h], place[3 + r, h]
        return total[upper : upper + 1, :] + total[lower : lower + 1, :]

    return row


def gradient_kernel(
    positions_ref, ghost_ref, pair_nodes_ref, corner_ref, own_ref, back_ref, terms_ref, node_ref, *, dom_count, slot_count
):
    owned_rows = own_ref.shape[1]
    dom_here = lax.axis_index("dom")
    sub_count = ghost_ref.shape[0] // dom_count
    reach = (slot_count - 1) // 2
    pair_count = pair_nodes_ref.shape[0]
    ghost_rows = slot_count * sub_count

    def ghost_place(k):
        return lax.rem(dom_here - k + reach + dom_count, dom_count) * sub_count

    def ghost_row(r, h):
        k, t = divmod(h - owned_rows, sub_count)
        return ghost_ref[pl.ds(ghost_place(k) + t, 1), 0, r * LANES : (r + 1) * LANES]

    def tets_of_pairs(g):
        index = pair_nodes_ref[g * 8 : (g + 1) * 8, :]
        nodes = [jnp.zeros(index.shape, jnp.float32)] * 3
        nodes = gather_rows(position_row(positions_ref), 0, owned_rows, index, nodes)
        nodes = gather_rows(ghost_row, owned_rows, owned_rows + ghost_rows, index, nodes)
        for q in range(2):
            corners = [[None] * 4 for _ in range(3)]
            for n in range(4):
                first = q * pair_count + g * 8
                place = corner_ref[first : first + 8, n, :]
                for r in range(3):
                    corners[r][n] = lane_gather(nodes[r], place + q * BLOCK_ROWS)
            gradient = distortion_gradient(corners)
            for r in range(3):
                for m in range(3):
                    for s, part in enumerate(split_two(gradient[r][m + 1])):
                        terms_ref[m * 2 + q, pl.ds(g * 64 + s * 4 + r, 8, stride=8), :] = part

    def add_tets(p):
        empty = jnp.zeros((8, LANES), jnp.float32)
        blocks = [p, pair_count + p]
        base = [one_hot(corner_ref[b, 0:1, :], BLOCK_ROWS, -1.0) for b in blocks]
        hits, terms = [], []
        for m in range(3):
            for q in range(2):
                hit = row_equals(corner_ref[blocks[q], m + 1 : m + 2, :], BLOCK_ROWS)
                hits.append(jnp.where(hit, jnp.ones_like(base[q]), base[q]))
                part = terms_ref[m * 2 + q, p * 8 : (p + 1) * 8, :]
                part = jnp.concatenate([part, empty] if q == 0 else [empty, part], axis=0)
                terms.append(part.astype(jnp.bfloat16))
        sums = contract_lanes(jnp.concatenate(terms, axis=1), jnp.concatenate(hits, axis=1))
        sums = jnp.concatenate([sums[:8], sums[8:]], axis=1)
        node_ref[p * 8 : (p + 1) * 8, :] = sums + pltpu.roll(sums, 4, 0)

    for g in range(pair_count // 8):
        tets_of_pairs(g)
    for p in range(pair_count):
        add_tets(p)
    back_ref[...] = jnp.zeros(back_ref.shape, jnp.float32)
    row = column_sums(node_ref, pair_nodes_ref, owned_rows + ghost_rows)
    for r in range(3):
        for h in range(owned_rows):
            own_ref[r, h : h + 1, :] = row(r, h)
        for k in range(slot_count):
            for t in range(sub_count):
                place = ghost_place(k) + t
                back_ref[pl.ds(place, 1), 0, r * LANES : (r + 1) * LANES] = row(r, owned_rows + k * sub_count + t)


def moved_positions(positions_ref, mask_ref, own_ref, back_ref, list_ref, valid_ref, dom_count):
    dom_here = lax.axis_index("dom")
    slot_count, sub_count, width = list_ref.shape
    reach = (slot_count - 1) // 2
    owned_rows = own_ref.shape[1]
    left, right = [], []
    for k in range(slot_count):
        source = lax.rem(dom_here + k - reach + dom_count, dom_count) * sub_count
        for t in range(sub_count):
            index = list_ref[k, t : t + 1, :]
            valid = valid_ref[k, t : t + 1, :] > 0.0
            mask = row_equals(index >> 7, owned_rows)
            parts = []
            for r in range(3):
                row = back_ref[pl.ds(source + t, 1), 0, r * LANES : (r + 1) * LANES]
                parts.append(split_two(jnp.where(valid, row, 0.0)))
            left.append(jnp.concatenate([masked_rows(mask, parts[r][s]) for s in range(2) for r in range(3)], axis=0))
            right.append(one_hot(index & (LANES - 1), LANES))
    returned = contract_lanes(jnp.concatenate(left, axis=1), jnp.concatenate(right, axis=1))
    free = jnp.where(mask_ref[...] == 0, step_size, 0.0)
    moved = []
    for r in range(3):
        added = returned[r * owned_rows : (r + 1) * owned_rows] + returned[(3 + r) * owned_rows : (4 + r) * owned_rows]
        here = jnp.concatenate(
            [positions_ref[r : r + 1, h * LANES : (h + 1) * LANES] for h in range(owned_rows)], axis=0
        )
        moved.append(here - free * (own_ref[r] + added))
    return moved


def move_kernel(positions_ref, mask_ref, own_ref, back_ref, list_ref, valid_ref, *out_refs, dom_count):
    moved = moved_positions(positions_ref, mask_ref, own_ref, back_ref, list_ref, valid_ref, dom_count)
    owned_rows = own_ref.shape[1]
    for r in range(3):
        for h in range(owned_rows):
            out_refs[0][r : r + 1, h * LANES : (h + 1) * LANES] = moved[r][h : h + 1]
    if len(out_refs) > 1:
        write_payload(lambda r, h: moved[r][h : h + 1], owned_rows, list_ref, valid_ref, out_refs[1], dom_count)


def per_device(positions, fixed_mask, send_count, send_list, block_nodes, tet_corners):
    node_count = positions.shape[1]
    slot_count, sub_count, width = send_list.shape[2:]
    dom_count = lax.axis_size("dom")
    block_count = block_nodes.shape[1]
    owned_rows = node_count // LANES
    counts = send_count[0, 0].T
    lists = send_list[0, 0]
    mask_rows = fixed_mask.reshape(owned_rows, LANES)
    corners = tet_corners.reshape(4, block_count, LANES).transpose(1, 0, 2)

    vmem = pl.BlockSpec(memory_space=pltpu.VMEM)
    hbm = pl.BlockSpec(memory_space=pl.ANY)
    exchange_shape = jax.ShapeDtypeStruct((dom_count * sub_count, 1, 3 * LANES), jnp.float32)
    position_shape = jax.ShapeDtypeStruct(positions.shape, jnp.float32)
    params = pltpu.CompilerParams(vmem_limit_bytes=32 * 1024 * 1024)

    def call(kernel, name, ins, outs, scratch=(), **sizes):
        return pl.pallas_call(
            functools.partial(kernel, **sizes),
            out_shape=outs,
            in_specs=ins,
            out_specs=jax.tree.map(lambda _: vmem, outs),
            scratch_shapes=scratch,
            compiler_params=params,
            name=name,
        )

    send = call(
        send_kernel,
        "send",
        [hbm] * 5,
        (
            exchange_shape,
            jax.ShapeDtypeStruct(lists.shape, jnp.float32),
            jax.ShapeDtypeStruct((block_count // 2, LANES), jnp.int32),
            jax.ShapeDtypeStruct(corners.shape, jnp.int32),
        ),
        [
            pltpu.VMEM(positions.shape, jnp.float32),
            pltpu.VMEM(lists.shape, jnp.int32),
            pltpu.VMEM(counts.shape, jnp.int32),
            pltpu.VMEM(block_nodes.shape, jnp.int32),
            pltpu.SemaphoreType.DMA((5,)),
        ],
        dom_count=dom_count,
    )
    own_shape = jax.ShapeDtypeStruct((3, owned_rows, LANES), jnp.float32)
    gradient = call(
        gradient_kernel,
        "gradient",
        [vmem] * 4,
        (own_shape, exchange_shape),
        [
            pltpu.VMEM((6, block_count * 4, LANES), jnp.float32),
            pltpu.VMEM((block_count * 4, LANES), jnp.float32),
        ],
        dom_count=dom_count,
        slot_count=slot_count,
    )

    def exchange(rows):
        return lax.all_to_all(rows, ("dom", "sub"), 0, 0, tiled=True)

    inputs = (positions, lists, counts, block_nodes, corners)
    payload, valid, pair_nodes, corners = send(*[pltpu.with_memory_space_constraint(x, pltpu.HBM) for x in inputs])
    for step in range(ITERS):
        last = step == ITERS - 1
        ghosts = exchange(payload)
        own, back = gradient(positions, ghosts, pair_nodes, corners)
        returned = exchange(back)
        move = call(
            move_kernel,
            "move_last" if last else "move",
            [vmem] * 6,
            (position_shape,) if last else (position_shape, exchange_shape),
            dom_count=dom_count,
        )
        moved = move(positions, mask_rows, own, returned, lists, valid)
        positions = moved[0]
        if not last:
            payload = moved[1]
    return positions


def solution(mesh):
    return jax.shard_map(
        per_device,
        mesh=mesh,
        in_specs=(
            P(None, ("dom", "sub")),
            P(("dom", "sub")),
            P("dom", "sub", None, None),
            P("dom", "sub", None, None, None),
            P(None, ("dom", "sub")),
            P(None, ("dom", "sub")),
        ),
        out_specs=P(None, ("dom", "sub")),
        check_vma=False,
    )
```

```python
import functools
import math

import jax
import jax.numpy as jnp
from jax import lax
from jax.experimental import pallas as pl
from jax.experimental.pallas import tpu as pltpu
from jax.sharding import PartitionSpec as P

ITERS = 2
LANES = 128
BLOCK_ROWS = 64

delta_reg = 2.0
step_size = 0.01

LANE_GATHER = lax.GatherDimensionNumbers(
    offset_dims=(),
    collapsed_slice_dims=(1,),
    start_index_map=(1,),
    operand_batching_dims=(0,),
    start_indices_batching_dims=(0,),
)


def lane_gather(table, index):
    return lax.gather(
        table,
        index[:, :, None],
        LANE_GATHER,
        slice_sizes=(1, 1),
        mode=lax.GatherScatterMode.PROMISE_IN_BOUNDS,
    )


def row_iota(rows):
    return lax.broadcasted_iota(jnp.int32, (rows, LANES), 0).astype(jnp.float32).astype(jnp.bfloat16)


def row_equals(ids_row, rows):
    packed = jnp.broadcast_to(ids_row, (16, LANES)).astype(jnp.int16)
    return jnp.concatenate([packed] * (rows // 16), axis=0) == lax.broadcasted_iota(jnp.int32, (rows, LANES), 0).astype(jnp.int16)


def one_hot(ids_row, rows, value=1.0):
    mask = row_equals(ids_row, rows)
    return jnp.where(mask, jnp.full((rows, LANES), value, jnp.bfloat16), jnp.zeros((rows, LANES), jnp.bfloat16))


def split_two(values):
    upper = values.astype(jnp.bfloat16).astype(jnp.float32)
    return upper, values - upper


def masked_rows(mask, row):
    rows = mask.shape[0]
    packed = jnp.broadcast_to(row, (16, LANES)).astype(jnp.bfloat16)
    tiled = jnp.concatenate([packed] * (rows // 16), axis=0)
    return jnp.where(mask, tiled, jnp.zeros((rows, LANES), jnp.bfloat16))


def contract_lanes(a, b):
    return lax.dot_general(a, b, (((1,), (1,)), ((), ())), preferred_element_type=jnp.float32)


def gather_rows(row_of, first, last, index, out):
    low = index & (LANES - 1)
    high = index >> 7
    out = list(out)
    for h in range(first, last):
        hit = high == h
        for r in range(3):
            table = jnp.broadcast_to(row_of(r, h), index.shape)
            out[r] = jnp.where(hit, lane_gather(table, low), out[r])
    return out


def distortion_gradient(corners):
    edge = [[corners[r][m + 1] - corners[r][0] for m in range(3)] for r in range(3)]
    half = [0.5 * (edge[r][0] + edge[r][1] + edge[r][2]) for r in range(3)]
    bent = [[2.0 * edge[r][m] - half[r] for m in range(3)] for r in range(3)]
    norm_sq = None
    for r in range(3):
        for m in range(3):
            term = edge[r][m] * bent[r][m]
            norm_sq = term if norm_sq is None else norm_sq + term
    cof = [[None] * 3 for _ in range(3)]
    for r in range(3):
        r1, r2 = (r + 1) % 3, (r + 2) % 3
        for m in range(3):
            m1, m2 = (m + 1) % 3, (m + 2) % 3
            cof[r][m] = edge[r1][m1] * edge[r2][m2] - edge[r1][m2] * edge[r2][m1]
    root2 = math.sqrt(2.0)
    volume_det = root2 * (edge[0][0] * cof[0][0] + edge[0][1] * cof[0][1] + edge[0][2] * cof[0][2])
    root_term = jnp.sqrt(volume_det * volume_det + 4.0 * delta_reg * delta_reg)
    spread = root_term + jnp.abs(volume_det)
    height = jnp.where(volume_det >= 0, 0.5 * spread, 2.0 * delta_reg * delta_reg / spread)
    outer = (2.0 / 3.0) * jnp.exp((-2.0 / 3.0) * jnp.log(height))
    inner = norm_sq * (root2 / 3.0) / root_term
    gradient = [[None] * 4 for _ in range(3)]
    for r in range(3):
        for m in range(3):
            gradient[r][m + 1] = outer * (bent[r][m] - inner * cof[r][m])
        gradient[r][0] = -(gradient[r][1] + gradient[r][2] + gradient[r][3])
    return gradient


def position_row(positions_ref):
    return lambda r, h: positions_ref[r : r + 1, h * LANES : (h + 1) * LANES]


def write_payload(row_of, owned_rows, list_ref, valid_ref, out_ref, dom_count):
    dom_here = lax.axis_index("dom")
    slot_count, sub_count, width = list_ref.shape
    reach = (slot_count - 1) // 2
    out_ref[...] = jnp.zeros(out_ref.shape, jnp.float32)
    group = max(1, 8 // sub_count)
    for first in range(0, slot_count, group):
        slots = range(first, min(first + group, slot_count))
        index = jnp.concatenate([list_ref[k] for k in slots], axis=0)
        valid = jnp.concatenate([valid_ref[k] for k in slots], axis=0)
        zeros = [jnp.zeros(index.shape, jnp.float32)] * 3
        picked = [x * valid for x in gather_rows(row_of, 0, owned_rows, index, zeros)]
        for i, k in enumerate(slots):
            target = lax.rem(dom_here + k - reach + dom_count, dom_count) * sub_count
            for t in range(sub_count):
                for r in range(3):
                    row = picked[r][i * sub_count + t : i * sub_count + t + 1, :]
                    out_ref[pl.ds(target + t, 1), 0, r * LANES : (r + 1) * LANES] = row


def send_kernel(
    positions_hbm,
    list_hbm,
    count_hbm,
    block_nodes_hbm,
    corner_hbm,
    out_ref,
    valid_ref,
    pair_nodes_ref,
    block_nodes_ref,
    corner_ref,
    positions_ref,
    list_ref,
    count_ref,
    sems,
    *,
    dom_count,
):
    copies = [
        pltpu.make_async_copy(source, target, sems.at[i])
        for i, (source, target) in enumerate(
            [
                (positions_hbm, positions_ref),
                (list_hbm, list_ref),
                (count_hbm, count_ref),
                (block_nodes_hbm, block_nodes_ref),
                (corner_hbm, corner_ref),
            ]
        )
    ]
    for copy in copies:
        copy.start()
    for copy in copies[:3]:
        copy.wait()
    slot_count, sub_count, width = list_ref.shape
    lane = lax.broadcasted_iota(jnp.int32, (sub_count, LANES), 1)
    for k in range(slot_count):
        counts = jnp.broadcast_to(count_ref[:, k : k + 1], (sub_count, LANES))
        valid_ref[k] = jnp.where(lane < counts, 1.0, 0.0)
    write_payload(
        position_row(positions_ref), positions_ref.shape[1] // LANES, list_ref, valid_ref, out_ref, dom_count
    )
    copies[3].wait()
    half = pair_nodes_ref.shape[0]
    nodes = block_nodes_ref[...].T
    pair_nodes_ref[...] = jnp.concatenate([nodes[:half], nodes[half:]], axis=1)
    copies[4].wait()


def spread_rows(high_row, parts, rows):
    tiles, place = [], {}
    full, rest = divmod(rows, 16)
    parts = [jnp.broadcast_to(part, (16, LANES)).astype(jnp.bfloat16) for part in parts]
    high = jnp.broadcast_to(high_row, (16, LANES)).astype(jnp.bfloat16)
    zero = jnp.zeros((16, LANES), jnp.bfloat16)
    row = lax.broadcasted_iota(jnp.int32, (16, LANES), 0)
    for f in range(full):
        mask = high == (row + 16 * f).astype(jnp.float32).astype(jnp.bfloat16)
        for i, part in enumerate(parts):
            place.update({(i, 16 * f + h): len(tiles) * 16 + h for h in range(16)})
            tiles.append(jnp.where(mask, part, zero))
    if rest:
        share = 16 // rest
        masks = []
        for j in range(share):
            wanted = jnp.where((row >= j * rest) & (row < (j + 1) * rest), row - j * rest + 16 * full, -1)
            masks.append(high == wanted.astype(jnp.float32).astype(jnp.bfloat16))
        for first in range(0, len(parts), share):
            tile = zero
            for j, i in enumerate(range(first, min(first + share, len(parts)))):
                place.update({(i, 16 * full + h): len(tiles) * 16 + j * rest + h for h in range(rest)})
                tile = jnp.where(masks[j], parts[i], tile)
            tiles.append(tile)
    return jnp.concatenate(tiles, axis=0), place


def column_sums(node_ref, pair_nodes_ref, block_nodes_ref, rows):
    pair_count = pair_nodes_ref.shape[0]
    left, right = [], []
    place = None
    low = (block_nodes_ref[...] & (2 * LANES - 1)).astype(jnp.int16)
    lane = lax.broadcasted_iota(jnp.int32, (BLOCK_ROWS, LANES), 1)
    lanes = [(lane + i * LANES).astype(jnp.int16) for i in range(2)]
    ones = jnp.ones((BLOCK_ROWS, LANES), jnp.bfloat16)
    for p in range(pair_count):
        parts = [part[r : r + 1, :] for part in split_two(node_ref[p * 8 : (p + 1) * 8, :]) for r in range(3)]
        high = pair_nodes_ref[p : p + 1, :] >> 8
        spread, place = spread_rows(high.astype(jnp.float32), parts, -(-rows // 2))
        left.append(spread)
        for b in (p, pair_count + p):
            column = jnp.broadcast_to(low[:, b : b + 1], (BLOCK_ROWS, LANES))
            halves = [jnp.where(column == half, ones, jnp.zeros_like(ones)) for half in lanes]
            right.append(jnp.concatenate(halves, axis=1))
    total = lax.dot_general(
        jnp.concatenate(left, axis=1),
        jnp.concatenate(right, axis=0),
        (((1,), (0,)), ((), ())),
        preferred_element_type=jnp.float32,
    )

    def row(r, h):
        upper, lower = place[r, h // 2], place[3 + r, h // 2]
        half = slice((h % 2) * LANES, (h % 2 + 1) * LANES)
        return total[upper : upper + 1, half] + total[lower : lower + 1, half]

    return row


def gradient_kernel(
    positions_ref, ghost_ref, pair_nodes_ref, block_nodes_ref, corner_ref, own_ref, back_ref, terms_ref, node_ref, *, dom_count, slot_count
):
    owned_rows = own_ref.shape[1]
    dom_here = lax.axis_index("dom")
    sub_count = ghost_ref.shape[0] // dom_count
    reach = (slot_count - 1) // 2
    pair_count = pair_nodes_ref.shape[0]
    ghost_rows = slot_count * sub_count

    def ghost_place(k):
        return lax.rem(dom_here - k + reach + dom_count, dom_count) * sub_count

    def ghost_row(r, h):
        k, t = divmod(h - owned_rows, sub_count)
        return ghost_ref[pl.ds(ghost_place(k) + t, 1), 0, r * LANES : (r + 1) * LANES]

    def tets_of_pairs(g):
        index = pair_nodes_ref[g * 8 : (g + 1) * 8, :]
        nodes = [jnp.zeros(index.shape, jnp.float32)] * 3
        nodes = gather_rows(position_row(positions_ref), 0, owned_rows, index, nodes)
        nodes = gather_rows(ghost_row, owned_rows, owned_rows + ghost_rows, index, nodes)
        for q in range(2):
            corners = [[None] * 4 for _ in range(3)]
            for n in range(4):
                first = q * pair_count + g * 8
                place = corner_ref[first : first + 8, n, :]
                for r in range(3):
                    corners[r][n] = lane_gather(nodes[r], place + q * BLOCK_ROWS)
            gradient = distortion_gradient(corners)
            for r in range(3):
                for m in range(3):
                    for s, part in enumerate(split_two(gradient[r][m + 1])):
                        terms_ref[m * 2 + q, pl.ds(g * 64 + s * 4 + r, 8, stride=8), :] = part

    def add_tets(p):
        empty = jnp.zeros((8, LANES), jnp.float32)
        blocks = [p, pair_count + p]
        base = [one_hot(corner_ref[b, 0:1, :], BLOCK_ROWS, -1.0) for b in blocks]
        hits, terms = [], []
        for m in range(3):
            for q in range(2):
                hit = row_equals(corner_ref[blocks[q], m + 1 : m + 2, :], BLOCK_ROWS)
                hits.append(jnp.where(hit, jnp.ones_like(base[q]), base[q]))
                part = terms_ref[m * 2 + q, p * 8 : (p + 1) * 8, :]
                part = jnp.concatenate([part, empty] if q == 0 else [empty, part], axis=0)
                terms.append(part.astype(jnp.bfloat16))
        sums = contract_lanes(jnp.concatenate(terms, axis=1), jnp.concatenate(hits, axis=1))
        sums = jnp.concatenate([sums[:8], sums[8:]], axis=1)
        node_ref[p * 8 : (p + 1) * 8, :] = sums + pltpu.roll(sums, 4, 0)

    for g in range(pair_count // 8):
        tets_of_pairs(g)
    for p in range(pair_count):
        add_tets(p)
    back_ref[...] = jnp.zeros(back_ref.shape, jnp.float32)
    row = column_sums(node_ref, pair_nodes_ref, block_nodes_ref, owned_rows + ghost_rows)
    for r in range(3):
        for h in range(owned_rows):
            own_ref[r, h : h + 1, :] = row(r, h)
        for k in range(slot_count):
            for t in range(sub_count):
                place = ghost_place(k) + t
                back_ref[pl.ds(place, 1), 0, r * LANES : (r + 1) * LANES] = row(r, owned_rows + k * sub_count + t)


def moved_positions(positions_ref, mask_ref, own_ref, back_ref, list_ref, valid_ref, dom_count):
    dom_here = lax.axis_index("dom")
    slot_count, sub_count, width = list_ref.shape
    reach = (slot_count - 1) // 2
    owned_rows = own_ref.shape[1]
    left, right = [], []
    for k in range(slot_count):
        source = lax.rem(dom_here + k - reach + dom_count, dom_count) * sub_count
        for t in range(sub_count):
            index = list_ref[k, t : t + 1, :]
            valid = valid_ref[k, t : t + 1, :] > 0.0
            mask = row_equals(index >> 7, owned_rows)
            parts = []
            for r in range(3):
                row = back_ref[pl.ds(source + t, 1), 0, r * LANES : (r + 1) * LANES]
                parts.append(split_two(jnp.where(valid, row, 0.0)))
            left.append(jnp.concatenate([masked_rows(mask, parts[r][s]) for s in range(2) for r in range(3)], axis=0))
            right.append(one_hot(index & (LANES - 1), LANES))
    returned = contract_lanes(jnp.concatenate(left, axis=1), jnp.concatenate(right, axis=1))
    free = jnp.where(mask_ref[...] == 0, step_size, 0.0)
    moved = []
    for r in range(3):
        added = returned[r * owned_rows : (r + 1) * owned_rows] + returned[(3 + r) * owned_rows : (4 + r) * owned_rows]
        here = jnp.concatenate(
            [positions_ref[r : r + 1, h * LANES : (h + 1) * LANES] for h in range(owned_rows)], axis=0
        )
        moved.append(here - free * (own_ref[r] + added))
    return moved


def move_kernel(positions_ref, mask_ref, own_ref, back_ref, list_ref, valid_ref, *out_refs, dom_count):
    moved = moved_positions(positions_ref, mask_ref, own_ref, back_ref, list_ref, valid_ref, dom_count)
    owned_rows = own_ref.shape[1]
    for r in range(3):
        for h in range(owned_rows):
            out_refs[0][r : r + 1, h * LANES : (h + 1) * LANES] = moved[r][h : h + 1]
    if len(out_refs) > 1:
        write_payload(lambda r, h: moved[r][h : h + 1], owned_rows, list_ref, valid_ref, out_refs[1], dom_count)


def per_device(positions, fixed_mask, send_count, send_list, block_nodes, tet_corners):
    node_count = positions.shape[1]
    slot_count, sub_count, width = send_list.shape[2:]
    dom_count = lax.axis_size("dom")
    block_count = block_nodes.shape[1]
    owned_rows = node_count // LANES
    counts = send_count[0, 0].T
    lists = send_list[0, 0]
    mask_rows = fixed_mask.reshape(owned_rows, LANES)
    corners = tet_corners.reshape(4, block_count, LANES).transpose(1, 0, 2)

    vmem = pl.BlockSpec(memory_space=pltpu.VMEM)
    hbm = pl.BlockSpec(memory_space=pl.ANY)
    exchange_shape = jax.ShapeDtypeStruct((dom_count * sub_count, 1, 3 * LANES), jnp.float32)
    position_shape = jax.ShapeDtypeStruct(positions.shape, jnp.float32)
    params = pltpu.CompilerParams(vmem_limit_bytes=32 * 1024 * 1024)

    def call(kernel, name, ins, outs, scratch=(), **sizes):
        return pl.pallas_call(
            functools.partial(kernel, **sizes),
            out_shape=outs,
            in_specs=ins,
            out_specs=jax.tree.map(lambda _: vmem, outs),
            scratch_shapes=scratch,
            compiler_params=params,
            name=name,
        )

    send = call(
        send_kernel,
        "send",
        [hbm] * 5,
        (
            exchange_shape,
            jax.ShapeDtypeStruct(lists.shape, jnp.float32),
            jax.ShapeDtypeStruct((block_count // 2, LANES), jnp.int32),
            jax.ShapeDtypeStruct(block_nodes.shape, jnp.int32),
            jax.ShapeDtypeStruct(corners.shape, jnp.int32),
        ),
        [
            pltpu.VMEM(positions.shape, jnp.float32),
            pltpu.VMEM(lists.shape, jnp.int32),
            pltpu.VMEM(counts.shape, jnp.int32),
            pltpu.SemaphoreType.DMA((5,)),
        ],
        dom_count=dom_count,
    )
    own_shape = jax.ShapeDtypeStruct((3, owned_rows, LANES), jnp.float32)
    gradient = call(
        gradient_kernel,
        "gradient",
        [vmem] * 5,
        (own_shape, exchange_shape),
        [
            pltpu.VMEM((6, block_count * 4, LANES), jnp.float32),
            pltpu.VMEM((block_count * 4, LANES), jnp.float32),
        ],
        dom_count=dom_count,
        slot_count=slot_count,
    )

    def exchange(rows):
        return lax.all_to_all(rows, ("dom", "sub"), 0, 0, tiled=True)

    inputs = (positions, lists, counts, block_nodes, corners)
    payload, valid, pair_nodes, block_nodes, corners = send(*[pltpu.with_memory_space_constraint(x, pltpu.HBM) for x in inputs])
    for step in range(ITERS):
        last = step == ITERS - 1
        ghosts = exchange(payload)
        own, back = gradient(positions, ghosts, pair_nodes, block_nodes, corners)
        returned = exchange(back)
        move = call(
            move_kernel,
            "move_last" if last else "move",
            [vmem] * 6,
            (position_shape,) if last else (position_shape, exchange_shape),
            dom_count=dom_count,
        )
        moved = move(positions, mask_rows, own, returned, lists, valid)
        positions = moved[0]
        if not last:
            payload = moved[1]
    return positions


def solution(mesh):
    return jax.shard_map(
        per_device,
        mesh=mesh,
        in_specs=(
            P(None, ("dom", "sub")),
            P(("dom", "sub")),
            P("dom", "sub", None, None),
            P("dom", "sub", None, None, None),
            P(None, ("dom", "sub")),
            P(None, ("dom", "sub")),
        ),
        out_specs=P(None, ("dom", "sub")),
        check_vma=False,
    )
```

```python
import functools
import math

import jax
import jax.numpy as jnp
from jax import lax
from jax.experimental import pallas as pl
from jax.experimental.pallas import tpu as pltpu
from jax.sharding import PartitionSpec as P

ITERS = 2
LANES = 128
BLOCK_ROWS = 64

delta_reg = 2.0
step_size = 0.01

LANE_GATHER = lax.GatherDimensionNumbers(
    offset_dims=(),
    collapsed_slice_dims=(1,),
    start_index_map=(1,),
    operand_batching_dims=(0,),
    start_indices_batching_dims=(0,),
)


def lane_gather(table, index):
    return lax.gather(
        table,
        index[:, :, None],
        LANE_GATHER,
        slice_sizes=(1, 1),
        mode=lax.GatherScatterMode.PROMISE_IN_BOUNDS,
    )


def row_iota(rows):
    return lax.broadcasted_iota(jnp.int32, (rows, LANES), 0).astype(jnp.float32).astype(jnp.bfloat16)


def row_equals(ids_row, rows):
    packed = jnp.broadcast_to(ids_row, (16, LANES)).astype(jnp.int16)
    return jnp.concatenate([packed] * (rows // 16), axis=0) == lax.broadcasted_iota(jnp.int32, (rows, LANES), 0).astype(jnp.int16)


def one_hot(ids_row, rows, value=1.0):
    mask = row_equals(ids_row, rows)
    return jnp.where(mask, jnp.full((rows, LANES), value, jnp.bfloat16), jnp.zeros((rows, LANES), jnp.bfloat16))


def split(values, count):
    parts = []
    for _ in range(count - 1):
        upper = values.astype(jnp.bfloat16).astype(jnp.float32)
        parts.append(upper)
        values = values - upper
    return parts + [values]


def masked_rows(mask, row):
    rows = mask.shape[0]
    packed = jnp.broadcast_to(row, (16, LANES)).astype(jnp.bfloat16)
    tiled = jnp.concatenate([packed] * (rows // 16), axis=0)
    return jnp.where(mask, tiled, jnp.zeros((rows, LANES), jnp.bfloat16))


def contract_lanes(a, b):
    return lax.dot_general(a, b, (((1,), (1,)), ((), ())), preferred_element_type=jnp.float32)


def gather_rows(row_of, first, last, index, out):
    low = index & (LANES - 1)
    high = index >> 7
    out = list(out)
    for h in range(first, last):
        hit = high == h
        for r in range(3):
            table = jnp.broadcast_to(row_of(r, h), index.shape)
            out[r] = jnp.where(hit, lane_gather(table, low), out[r])
    return out


def distortion_gradient(corners):
    edge = [[corners[r][m + 1] - corners[r][0] for m in range(3)] for r in range(3)]
    half = [0.5 * (edge[r][0] + edge[r][1] + edge[r][2]) for r in range(3)]
    bent = [[2.0 * edge[r][m] - half[r] for m in range(3)] for r in range(3)]
    norm_sq = None
    for r in range(3):
        for m in range(3):
            term = edge[r][m] * bent[r][m]
            norm_sq = term if norm_sq is None else norm_sq + term
    cof = [[None] * 3 for _ in range(3)]
    for r in range(3):
        r1, r2 = (r + 1) % 3, (r + 2) % 3
        for m in range(3):
            m1, m2 = (m + 1) % 3, (m + 2) % 3
            cof[r][m] = edge[r1][m1] * edge[r2][m2] - edge[r1][m2] * edge[r2][m1]
    root2 = math.sqrt(2.0)
    volume_det = root2 * (edge[0][0] * cof[0][0] + edge[0][1] * cof[0][1] + edge[0][2] * cof[0][2])
    root_term = jnp.sqrt(volume_det * volume_det + 4.0 * delta_reg * delta_reg)
    spread = root_term + jnp.abs(volume_det)
    height = jnp.where(volume_det >= 0, 0.5 * spread, 2.0 * delta_reg * delta_reg / spread)
    outer = (2.0 / 3.0) * jnp.exp((-2.0 / 3.0) * jnp.log(height))
    inner = norm_sq * (root2 / 3.0) / root_term
    gradient = [[None] * 4 for _ in range(3)]
    for r in range(3):
        for m in range(3):
            gradient[r][m + 1] = outer * (bent[r][m] - inner * cof[r][m])
        gradient[r][0] = -(gradient[r][1] + gradient[r][2] + gradient[r][3])
    return gradient


def position_row(positions_ref):
    return lambda r, h: positions_ref[r : r + 1, h * LANES : (h + 1) * LANES]


def write_payload(row_of, owned_rows, list_ref, valid_ref, out_ref, dom_count):
    dom_here = lax.axis_index("dom")
    slot_count, sub_count, width = list_ref.shape
    reach = (slot_count - 1) // 2
    out_ref[...] = jnp.zeros(out_ref.shape, jnp.float32)
    group = max(1, 8 // sub_count)
    for first in range(0, slot_count, group):
        slots = range(first, min(first + group, slot_count))
        index = jnp.concatenate([list_ref[k] for k in slots], axis=0)
        valid = jnp.concatenate([valid_ref[k] for k in slots], axis=0)
        zeros = [jnp.zeros(index.shape, jnp.float32)] * 3
        picked = [x * valid for x in gather_rows(row_of, 0, owned_rows, index, zeros)]
        for i, k in enumerate(slots):
            target = lax.rem(dom_here + k - reach + dom_count, dom_count) * sub_count
            for t in range(sub_count):
                for r in range(3):
                    row = picked[r][i * sub_count + t : i * sub_count + t + 1, :]
                    out_ref[pl.ds(target + t, 1), 0, r * LANES : (r + 1) * LANES] = row


def send_kernel(
    positions_hbm,
    list_hbm,
    count_hbm,
    block_nodes_hbm,
    corner_hbm,
    out_ref,
    valid_ref,
    pair_nodes_ref,
    block_nodes_ref,
    corner_ref,
    positions_ref,
    list_ref,
    count_ref,
    sems,
    *,
    dom_count,
):
    copies = [
        pltpu.make_async_copy(source, target, sems.at[i])
        for i, (source, target) in enumerate(
            [
                (positions_hbm, positions_ref),
                (list_hbm, list_ref),
                (count_hbm, count_ref),
                (block_nodes_hbm, block_nodes_ref),
                (corner_hbm, corner_ref),
            ]
        )
    ]
    for copy in copies:
        copy.start()
    for copy in copies[:3]:
        copy.wait()
    slot_count, sub_count, width = list_ref.shape
    lane = lax.broadcasted_iota(jnp.int32, (sub_count, LANES), 1)
    for k in range(slot_count):
        counts = jnp.broadcast_to(count_ref[:, k : k + 1], (sub_count, LANES))
        valid_ref[k] = jnp.where(lane < counts, 1.0, 0.0)
    write_payload(
        position_row(positions_ref), positions_ref.shape[1] // LANES, list_ref, valid_ref, out_ref, dom_count
    )
    copies[3].wait()
    half = pair_nodes_ref.shape[0]
    nodes = block_nodes_ref[...].T
    pair_nodes_ref[...] = jnp.concatenate([nodes[:half], nodes[half:]], axis=1)
    copies[4].wait()


def spread_rows(high_row, parts, rows):
    tiles, place = [], {}
    full, rest = divmod(rows, 16)
    parts = [jnp.broadcast_to(part, (16, LANES)).astype(jnp.bfloat16) for part in parts]
    high = jnp.broadcast_to(high_row, (16, LANES)).astype(jnp.bfloat16)
    zero = jnp.zeros((16, LANES), jnp.bfloat16)
    row = lax.broadcasted_iota(jnp.int32, (16, LANES), 0)
    for f in range(full):
        mask = high == (row + 16 * f).astype(jnp.float32).astype(jnp.bfloat16)
        for i, part in enumerate(parts):
            place.update({(i, 16 * f + h): len(tiles) * 16 + h for h in range(16)})
            tiles.append(jnp.where(mask, part, zero))
    if rest:
        share = 16 // rest
        masks = []
        for j in range(share):
            wanted = jnp.where((row >= j * rest) & (row < (j + 1) * rest), row - j * rest + 16 * full, -1)
            masks.append(high == wanted.astype(jnp.float32).astype(jnp.bfloat16))
        for first in range(0, len(parts), share):
            tile = zero
            for j, i in enumerate(range(first, min(first + share, len(parts)))):
                place.update({(i, 16 * full + h): len(tiles) * 16 + j * rest + h for h in range(rest)})
                tile = jnp.where(masks[j], parts[i], tile)
            tiles.append(tile)
    return jnp.concatenate(tiles, axis=0), place


def column_sums(node_ref, pair_nodes_ref, block_nodes_ref, rows, splits):
    pair_count = pair_nodes_ref.shape[0]
    left, right = [], []
    place = None
    low = (block_nodes_ref[...] & (2 * LANES - 1)).astype(jnp.int16)
    lane = lax.broadcasted_iota(jnp.int32, (BLOCK_ROWS, LANES), 1)
    lanes = [(lane + i * LANES).astype(jnp.int16) for i in range(2)]
    ones = jnp.ones((BLOCK_ROWS, LANES), jnp.bfloat16)
    for p in range(pair_count):
        parts = [part[r : r + 1, :] for part in split(node_ref[p * 8 : (p + 1) * 8, :], splits) for r in range(3)]
        high = pair_nodes_ref[p : p + 1, :] >> 8
        spread, place = spread_rows(high.astype(jnp.float32), parts, -(-rows // 2))
        left.append(spread)
        for b in (p, pair_count + p):
            column = jnp.broadcast_to(low[:, b : b + 1], (BLOCK_ROWS, LANES))
            halves = [jnp.where(column == half, ones, jnp.zeros_like(ones)) for half in lanes]
            right.append(jnp.concatenate(halves, axis=1))
    total = lax.dot_general(
        jnp.concatenate(left, axis=1),
        jnp.concatenate(right, axis=0),
        (((1,), (0,)), ((), ())),
        preferred_element_type=jnp.float32,
    )

    def row(r, h):
        half = slice((h % 2) * LANES, (h % 2 + 1) * LANES)
        return sum(total[i : i + 1, half] for i in (place[3 * s + r, h // 2] for s in range(splits)))

    return row


def gradient_kernel(
    positions_ref, ghost_ref, pair_nodes_ref, block_nodes_ref, corner_ref, own_ref, back_ref, terms_ref, node_ref, *, dom_count, slot_count, splits
):
    part_rows = terms_ref.shape[1] // pair_nodes_ref.shape[0]
    owned_rows = own_ref.shape[1]
    dom_here = lax.axis_index("dom")
    sub_count = ghost_ref.shape[0] // dom_count
    reach = (slot_count - 1) // 2
    pair_count = pair_nodes_ref.shape[0]
    ghost_rows = slot_count * sub_count

    def ghost_place(k):
        return lax.rem(dom_here - k + reach + dom_count, dom_count) * sub_count

    def ghost_row(r, h):
        k, t = divmod(h - owned_rows, sub_count)
        return ghost_ref[pl.ds(ghost_place(k) + t, 1), 0, r * LANES : (r + 1) * LANES]

    def tets_of_pairs(g):
        index = pair_nodes_ref[g * 8 : (g + 1) * 8, :]
        nodes = [jnp.zeros(index.shape, jnp.float32)] * 3
        nodes = gather_rows(position_row(positions_ref), 0, owned_rows, index, nodes)
        nodes = gather_rows(ghost_row, owned_rows, owned_rows + ghost_rows, index, nodes)
        for q in range(2):
            corners = [[None] * 4 for _ in range(3)]
            for n in range(4):
                first = q * pair_count + g * 8
                place = corner_ref[first : first + 8, n, :]
                for r in range(3):
                    corners[r][n] = lane_gather(nodes[r], place + q * BLOCK_ROWS)
            gradient = distortion_gradient(corners)
            for r in range(3):
                for m in range(3):
                    for s, part in enumerate(split(gradient[r][m + 1], splits)):
                        first = g * 8 * part_rows + s * 4 + r
                        terms_ref[m * 2 + q, pl.ds(first, 8, stride=part_rows), :] = part

    def add_tets(p):
        empty = jnp.zeros((part_rows, LANES), jnp.float32)
        blocks = [p, pair_count + p]
        base = [one_hot(corner_ref[b, 0:1, :], BLOCK_ROWS, -1.0) for b in blocks]
        hits, terms = [], []
        for m in range(3):
            for q in range(2):
                hit = row_equals(corner_ref[blocks[q], m + 1 : m + 2, :], BLOCK_ROWS)
                hits.append(jnp.where(hit, jnp.ones_like(base[q]), base[q]))
                part = terms_ref[m * 2 + q, p * part_rows : (p + 1) * part_rows, :]
                part = jnp.concatenate([part, empty] if q == 0 else [empty, part], axis=0)
                terms.append(part.astype(jnp.bfloat16))
        sums = contract_lanes(jnp.concatenate(terms, axis=1), jnp.concatenate(hits, axis=1))
        sums = jnp.concatenate([sums[:part_rows], sums[part_rows:]], axis=1)
        node = sums[:8] + pltpu.roll(sums[:8], 4, 0)
        node_ref[p * 8 : (p + 1) * 8, :] = node + sums[8:] if part_rows > 8 else node

    for g in range(pair_count // 8):
        tets_of_pairs(g)
    for p in range(pair_count):
        add_tets(p)
    back_ref[...] = jnp.zeros(back_ref.shape, jnp.float32)
    row = column_sums(node_ref, pair_nodes_ref, block_nodes_ref, owned_rows + ghost_rows, splits)
    for r in range(3):
        for h in range(owned_rows):
            own_ref[r, h : h + 1, :] = row(r, h)
        for k in range(slot_count):
            for t in range(sub_count):
                place = ghost_place(k) + t
                back_ref[pl.ds(place, 1), 0, r * LANES : (r + 1) * LANES] = row(r, owned_rows + k * sub_count + t)


def moved_positions(positions_ref, mask_ref, own_ref, back_ref, list_ref, valid_ref, dom_count, splits):
    dom_here = lax.axis_index("dom")
    slot_count, sub_count, width = list_ref.shape
    reach = (slot_count - 1) // 2
    owned_rows = own_ref.shape[1]
    left, right = [], []
    for k in range(slot_count):
        source = lax.rem(dom_here + k - reach + dom_count, dom_count) * sub_count
        for t in range(sub_count):
            index = list_ref[k, t : t + 1, :]
            valid = valid_ref[k, t : t + 1, :] > 0.0
            mask = row_equals(index >> 7, owned_rows)
            parts = []
            for r in range(3):
                row = back_ref[pl.ds(source + t, 1), 0, r * LANES : (r + 1) * LANES]
                parts.append(split(jnp.where(valid, row, 0.0), splits))
            left.append(jnp.concatenate([masked_rows(mask, parts[r][s]) for s in range(splits) for r in range(3)], axis=0))
            right.append(one_hot(index & (LANES - 1), LANES))
    returned = contract_lanes(jnp.concatenate(left, axis=1), jnp.concatenate(right, axis=1))
    free = jnp.where(mask_ref[...] == 0, step_size, 0.0)
    moved = []
    for r in range(3):
        added = sum(returned[i * owned_rows : (i + 1) * owned_rows] for i in range(r, 3 * splits, 3))
        here = jnp.concatenate(
            [positions_ref[r : r + 1, h * LANES : (h + 1) * LANES] for h in range(owned_rows)], axis=0
        )
        moved.append(here - free * (own_ref[r] + added))
    return moved


def move_kernel(positions_ref, mask_ref, own_ref, back_ref, list_ref, valid_ref, *out_refs, dom_count, splits):
    moved = moved_positions(positions_ref, mask_ref, own_ref, back_ref, list_ref, valid_ref, dom_count, splits)
    owned_rows = own_ref.shape[1]
    for r in range(3):
        for h in range(owned_rows):
            out_refs[0][r : r + 1, h * LANES : (h + 1) * LANES] = moved[r][h : h + 1]
    if len(out_refs) > 1:
        write_payload(lambda r, h: moved[r][h : h + 1], owned_rows, list_ref, valid_ref, out_refs[1], dom_count)


def per_device(positions, fixed_mask, send_count, send_list, block_nodes, tet_corners):
    node_count = positions.shape[1]
    slot_count, sub_count, width = send_list.shape[2:]
    dom_count = lax.axis_size("dom")
    block_count = block_nodes.shape[1]
    owned_rows = node_count // LANES
    counts = send_count[0, 0].T
    lists = send_list[0, 0]
    mask_rows = fixed_mask.reshape(owned_rows, LANES)
    corners = tet_corners.reshape(4, block_count, LANES).transpose(1, 0, 2)

    vmem = pl.BlockSpec(memory_space=pltpu.VMEM)
    hbm = pl.BlockSpec(memory_space=pl.ANY)
    exchange_shape = jax.ShapeDtypeStruct((dom_count * sub_count, 1, 3 * LANES), jnp.float32)
    position_shape = jax.ShapeDtypeStruct(positions.shape, jnp.float32)
    params = pltpu.CompilerParams(vmem_limit_bytes=32 * 1024 * 1024)

    def call(kernel, name, ins, outs, scratch=(), **sizes):
        return pl.pallas_call(
            functools.partial(kernel, **sizes),
            out_shape=outs,
            in_specs=ins,
            out_specs=jax.tree.map(lambda _: vmem, outs),
            scratch_shapes=scratch,
            compiler_params=params,
            name=name,
        )

    send = call(
        send_kernel,
        "send",
        [hbm] * 5,
        (
            exchange_shape,
            jax.ShapeDtypeStruct(lists.shape, jnp.float32),
            jax.ShapeDtypeStruct((block_count // 2, LANES), jnp.int32),
            jax.ShapeDtypeStruct(block_nodes.shape, jnp.int32),
            jax.ShapeDtypeStruct(corners.shape, jnp.int32),
        ),
        [
            pltpu.VMEM(positions.shape, jnp.float32),
            pltpu.VMEM(lists.shape, jnp.int32),
            pltpu.VMEM(counts.shape, jnp.int32),
            pltpu.SemaphoreType.DMA((5,)),
        ],
        dom_count=dom_count,
    )
    own_shape = jax.ShapeDtypeStruct((3, owned_rows, LANES), jnp.float32)

    def exchange(rows):
        return lax.all_to_all(rows, ("dom", "sub"), 0, 0, tiled=True)

    inputs = (positions, lists, counts, block_nodes, corners)
    payload, valid, pair_nodes, block_nodes, corners = send(*[pltpu.with_memory_space_constraint(x, pltpu.HBM) for x in inputs])
    for step in range(ITERS):
        last = step == ITERS - 1
        ghosts = exchange(payload)
        splits = 2 if last else 3
        gradient = call(
            gradient_kernel,
            "gradient_last" if last else "gradient",
            [vmem] * 5,
            (own_shape, exchange_shape),
            [
                pltpu.VMEM((6, block_count * (4 if last else 8), LANES), jnp.float32),
                pltpu.VMEM((block_count * 4, LANES), jnp.float32),
            ],
            dom_count=dom_count,
            slot_count=slot_count,
            splits=splits,
        )
        own, back = gradient(positions, ghosts, pair_nodes, block_nodes, corners)
        returned = exchange(back)
        move = call(
            move_kernel,
            "move_last" if last else "move",
            [vmem] * 6,
            (position_shape,) if last else (position_shape, exchange_shape),
            dom_count=dom_count,
            splits=splits,
        )
        moved = move(positions, mask_rows, own, returned, lists, valid)
        positions = moved[0]
        if not last:
            payload = moved[1]
    return positions


def solution(mesh):
    return jax.shard_map(
        per_device,
        mesh=mesh,
        in_specs=(
            P(None, ("dom", "sub")),
            P(("dom", "sub")),
            P("dom", "sub", None, None),
            P("dom", "sub", None, None, None),
            P(None, ("dom", "sub")),
            P(None, ("dom", "sub")),
        ),
        out_specs=P(None, ("dom", "sub")),
        check_vma=False,
    )
```

```python
import functools
import math

import jax
import jax.numpy as jnp
from jax import lax
from jax.experimental import pallas as pl
from jax.experimental.pallas import tpu as pltpu
from jax.sharding import PartitionSpec as P

ITERS = 2
LANES = 128
BLOCK_ROWS = 64

delta_reg = 2.0
step_size = 0.01

LANE_GATHER = lax.GatherDimensionNumbers(
    offset_dims=(),
    collapsed_slice_dims=(1,),
    start_index_map=(1,),
    operand_batching_dims=(0,),
    start_indices_batching_dims=(0,),
)


def lane_gather(table, index):
    return lax.gather(
        table,
        index[:, :, None],
        LANE_GATHER,
        slice_sizes=(1, 1),
        mode=lax.GatherScatterMode.PROMISE_IN_BOUNDS,
    )


def row_iota(rows):
    return lax.broadcasted_iota(jnp.int32, (rows, LANES), 0).astype(jnp.float32).astype(jnp.bfloat16)


def row_equals(ids_row, rows):
    packed = jnp.broadcast_to(ids_row, (16, LANES)).astype(jnp.int16)
    return jnp.concatenate([packed] * (rows // 16), axis=0) == lax.broadcasted_iota(jnp.int32, (rows, LANES), 0).astype(jnp.int16)


def one_hot(ids_row, rows, value=1.0):
    mask = row_equals(ids_row, rows)
    return jnp.where(mask, jnp.full((rows, LANES), value, jnp.bfloat16), jnp.zeros((rows, LANES), jnp.bfloat16))


def split(values, count):
    parts = []
    for _ in range(count - 1):
        upper = values.astype(jnp.bfloat16).astype(jnp.float32)
        parts.append(upper)
        values = values - upper
    return parts + [values]


def masked_rows(mask, row):
    rows = mask.shape[0]
    packed = jnp.broadcast_to(row, (16, LANES)).astype(jnp.bfloat16)
    tiled = jnp.concatenate([packed] * (rows // 16), axis=0)
    return jnp.where(mask, tiled, jnp.zeros((rows, LANES), jnp.bfloat16))


def contract_lanes(a, b):
    return lax.dot_general(a, b, (((1,), (1,)), ((), ())), preferred_element_type=jnp.float32)


def gather_rows(row_of, first, last, index, out):
    low = index & (LANES - 1)
    high = index >> 7
    out = list(out)
    for h in range(first, last):
        hit = high == h
        for r in range(3):
            table = jnp.broadcast_to(row_of(r, h), index.shape)
            out[r] = jnp.where(hit, lane_gather(table, low), out[r])
    return out


def distortion_gradient(corners):
    edge = [[corners[r][m + 1] - corners[r][0] for m in range(3)] for r in range(3)]
    half = [0.5 * (edge[r][0] + edge[r][1] + edge[r][2]) for r in range(3)]
    bent = [[2.0 * edge[r][m] - half[r] for m in range(3)] for r in range(3)]
    norm_sq = None
    for r in range(3):
        for m in range(3):
            term = edge[r][m] * bent[r][m]
            norm_sq = term if norm_sq is None else norm_sq + term
    cof = [[None] * 3 for _ in range(3)]
    for r in range(3):
        r1, r2 = (r + 1) % 3, (r + 2) % 3
        for m in range(3):
            m1, m2 = (m + 1) % 3, (m + 2) % 3
            cof[r][m] = edge[r1][m1] * edge[r2][m2] - edge[r1][m2] * edge[r2][m1]
    root2 = math.sqrt(2.0)
    volume_det = root2 * (edge[0][0] * cof[0][0] + edge[0][1] * cof[0][1] + edge[0][2] * cof[0][2])
    root_term = jnp.sqrt(volume_det * volume_det + 4.0 * delta_reg * delta_reg)
    spread = root_term + jnp.abs(volume_det)
    height = jnp.where(volume_det >= 0, 0.5 * spread, 2.0 * delta_reg * delta_reg / spread)
    outer = (2.0 / 3.0) * jnp.exp((-2.0 / 3.0) * jnp.log(height))
    inner = norm_sq * (root2 / 3.0) / root_term
    gradient = [[None] * 4 for _ in range(3)]
    for r in range(3):
        for m in range(3):
            gradient[r][m + 1] = outer * (bent[r][m] - inner * cof[r][m])
        gradient[r][0] = -(gradient[r][1] + gradient[r][2] + gradient[r][3])
    return gradient


def position_row(positions_ref):
    return lambda r, h: positions_ref[r : r + 1, h * LANES : (h + 1) * LANES]


def write_payload(row_of, owned_rows, list_ref, valid_ref, out_ref, dom_count):
    dom_here = lax.axis_index("dom")
    slot_count, sub_count, width = list_ref.shape
    reach = (slot_count - 1) // 2
    group = max(1, 8 // sub_count)
    for first in range(0, slot_count, group):
        slots = range(first, min(first + group, slot_count))
        index = jnp.concatenate([list_ref[k] for k in slots], axis=0)
        valid = jnp.concatenate([valid_ref[k] for k in slots], axis=0)
        zeros = [jnp.zeros(index.shape, jnp.float32)] * 3
        picked = [x * valid for x in gather_rows(row_of, 0, owned_rows, index, zeros)]
        for i, k in enumerate(slots):
            target = lax.rem(dom_here + k - reach + dom_count, dom_count) * sub_count
            for t in range(sub_count):
                for r in range(3):
                    row = picked[r][i * sub_count + t : i * sub_count + t + 1, :]
                    out_ref[pl.ds(target + t, 1), 0, r * LANES : (r + 1) * LANES] = row


def send_kernel(
    positions_hbm,
    list_hbm,
    count_hbm,
    block_nodes_hbm,
    corner_hbm,
    out_ref,
    valid_ref,
    pair_nodes_ref,
    block_nodes_ref,
    corner_ref,
    positions_ref,
    list_ref,
    count_ref,
    sems,
    *,
    dom_count,
):
    copies = [
        pltpu.make_async_copy(source, target, sems.at[i])
        for i, (source, target) in enumerate(
            [
                (positions_hbm, positions_ref),
                (list_hbm, list_ref),
                (count_hbm, count_ref),
                (block_nodes_hbm, block_nodes_ref),
                (corner_hbm, corner_ref),
            ]
        )
    ]
    for copy in copies:
        copy.start()
    out_ref[...] = jnp.zeros(out_ref.shape, jnp.float32)
    for copy in copies[:4]:
        copy.wait()
    slot_count, sub_count, width = list_ref.shape
    lane = lax.broadcasted_iota(jnp.int32, (sub_count, LANES), 1)
    for k in range(slot_count):
        counts = jnp.broadcast_to(count_ref[:, k : k + 1], (sub_count, LANES))
        valid_ref[k] = jnp.where(lane < counts, 1.0, 0.0)
    write_payload(
        position_row(positions_ref), positions_ref.shape[1] // LANES, list_ref, valid_ref, out_ref, dom_count
    )
    half = pair_nodes_ref.shape[0]
    nodes = block_nodes_ref[...].T
    pair_nodes_ref[...] = jnp.concatenate([nodes[:half], nodes[half:]], axis=1)
    copies[4].wait()


def spread_rows(high_row, parts, rows):
    tiles, place = [], {}
    full, rest = divmod(rows, 16)
    parts = [jnp.broadcast_to(part, (16, LANES)).astype(jnp.bfloat16) for part in parts]
    high = jnp.broadcast_to(high_row, (16, LANES)).astype(jnp.bfloat16)
    zero = jnp.zeros((16, LANES), jnp.bfloat16)
    row = lax.broadcasted_iota(jnp.int32, (16, LANES), 0)
    for f in range(full):
        mask = high == (row + 16 * f).astype(jnp.float32).astype(jnp.bfloat16)
        for i, part in enumerate(parts):
            place.update({(i, 16 * f + h): len(tiles) * 16 + h for h in range(16)})
            tiles.append(jnp.where(mask, part, zero))
    if rest:
        share = 16 // rest
        masks = []
        for j in range(share):
            wanted = jnp.where((row >= j * rest) & (row < (j + 1) * rest), row - j * rest + 16 * full, -1)
            masks.append(high == wanted.astype(jnp.float32).astype(jnp.bfloat16))
        for first in range(0, len(parts), share):
            tile = zero
            for j, i in enumerate(range(first, min(first + share, len(parts)))):
                place.update({(i, 16 * full + h): len(tiles) * 16 + j * rest + h for h in range(rest)})
                tile = jnp.where(masks[j], parts[i], tile)
            tiles.append(tile)
    return jnp.concatenate(tiles, axis=0), place


def column_sums(node_ref, pair_nodes_ref, block_nodes_ref, rows, splits):
    pair_count = pair_nodes_ref.shape[0]
    left, right = [], []
    place = None
    low = (block_nodes_ref[...] & (2 * LANES - 1)).astype(jnp.int16)
    lane = lax.broadcasted_iota(jnp.int32, (BLOCK_ROWS, LANES), 1)
    lanes = [(lane + i * LANES).astype(jnp.int16) for i in range(2)]
    ones = jnp.ones((BLOCK_ROWS, LANES), jnp.bfloat16)
    for p in range(pair_count):
        parts = [part[r : r + 1, :] for part in split(node_ref[p * 8 : (p + 1) * 8, :], splits) for r in range(3)]
        high = pair_nodes_ref[p : p + 1, :] >> 8
        spread, place = spread_rows(high.astype(jnp.float32), parts, -(-rows // 2))
        left.append(spread)
        for b in (p, pair_count + p):
            column = jnp.broadcast_to(low[:, b : b + 1], (BLOCK_ROWS, LANES))
            halves = [jnp.where(column == half, ones, jnp.zeros_like(ones)) for half in lanes]
            right.append(jnp.concatenate(halves, axis=1))
    total = lax.dot_general(
        jnp.concatenate(left, axis=1),
        jnp.concatenate(right, axis=0),
        (((1,), (0,)), ((), ())),
        preferred_element_type=jnp.float32,
    )

    def row(r, h):
        half = slice((h % 2) * LANES, (h % 2 + 1) * LANES)
        return sum(total[i : i + 1, half] for i in (place[3 * s + r, h // 2] for s in range(splits)))

    return row


def gradient_kernel(
    positions_ref, ghost_ref, pair_nodes_ref, block_nodes_ref, corner_ref, own_ref, back_ref, terms_ref, node_ref, *, dom_count, slot_count, splits
):
    part_rows = terms_ref.shape[1] // pair_nodes_ref.shape[0]
    owned_rows = own_ref.shape[1]
    dom_here = lax.axis_index("dom")
    sub_count = ghost_ref.shape[0] // dom_count
    reach = (slot_count - 1) // 2
    pair_count = pair_nodes_ref.shape[0]
    ghost_rows = slot_count * sub_count

    def ghost_place(k):
        return lax.rem(dom_here - k + reach + dom_count, dom_count) * sub_count

    def ghost_row(r, h):
        k, t = divmod(h - owned_rows, sub_count)
        return ghost_ref[pl.ds(ghost_place(k) + t, 1), 0, r * LANES : (r + 1) * LANES]

    def tets_of_pairs(g):
        index = pair_nodes_ref[g * 8 : (g + 1) * 8, :]
        nodes = [jnp.zeros(index.shape, jnp.float32)] * 3
        nodes = gather_rows(position_row(positions_ref), 0, owned_rows, index, nodes)
        nodes = gather_rows(ghost_row, owned_rows, owned_rows + ghost_rows, index, nodes)
        for q in range(2):
            corners = [[None] * 4 for _ in range(3)]
            for n in range(4):
                first = q * pair_count + g * 8
                place = corner_ref[first : first + 8, n, :]
                for r in range(3):
                    corners[r][n] = lane_gather(nodes[r], place + q * BLOCK_ROWS)
            gradient = distortion_gradient(corners)
            for r in range(3):
                for m in range(3):
                    for s, part in enumerate(split(gradient[r][m + 1], splits)):
                        first = g * 8 * part_rows + s * 4 + r
                        terms_ref[m * 2 + q, pl.ds(first, 8, stride=part_rows), :] = part

    def add_tets(p):
        empty = jnp.zeros((part_rows, LANES), jnp.float32)
        blocks = [p, pair_count + p]
        base = [one_hot(corner_ref[b, 0:1, :], BLOCK_ROWS, -1.0) for b in blocks]
        hits, terms = [], []
        for m in range(3):
            for q in range(2):
                hit = row_equals(corner_ref[blocks[q], m + 1 : m + 2, :], BLOCK_ROWS)
                hits.append(jnp.where(hit, jnp.ones_like(base[q]), base[q]))
                part = terms_ref[m * 2 + q, p * part_rows : (p + 1) * part_rows, :]
                part = jnp.concatenate([part, empty] if q == 0 else [empty, part], axis=0)
                terms.append(part.astype(jnp.bfloat16))
        sums = contract_lanes(jnp.concatenate(terms, axis=1), jnp.concatenate(hits, axis=1))
        sums = jnp.concatenate([sums[:part_rows], sums[part_rows:]], axis=1)
        node = sums[:8] + pltpu.roll(sums[:8], 4, 0)
        node_ref[p * 8 : (p + 1) * 8, :] = node + sums[8:] if part_rows > 8 else node

    for g in range(pair_count // 8):
        tets_of_pairs(g)
    for p in range(pair_count):
        add_tets(p)
    back_ref[...] = jnp.zeros(back_ref.shape, jnp.float32)
    row = column_sums(node_ref, pair_nodes_ref, block_nodes_ref, owned_rows + ghost_rows, splits)
    for r in range(3):
        for h in range(owned_rows):
            own_ref[r, h : h + 1, :] = row(r, h)
        for k in range(slot_count):
            for t in range(sub_count):
                place = ghost_place(k) + t
                back_ref[pl.ds(place, 1), 0, r * LANES : (r + 1) * LANES] = row(r, owned_rows + k * sub_count + t)


def moved_positions(positions_ref, mask_ref, own_ref, back_ref, list_ref, valid_ref, dom_count, splits):
    dom_here = lax.axis_index("dom")
    slot_count, sub_count, width = list_ref.shape
    reach = (slot_count - 1) // 2
    owned_rows = own_ref.shape[1]
    left, right = [], []
    for k in range(slot_count):
        source = lax.rem(dom_here + k - reach + dom_count, dom_count) * sub_count
        for t in range(sub_count):
            index = list_ref[k, t : t + 1, :]
            valid = valid_ref[k, t : t + 1, :] > 0.0
            mask = row_equals(index >> 7, owned_rows)
            parts = []
            for r in range(3):
                row = back_ref[pl.ds(source + t, 1), 0, r * LANES : (r + 1) * LANES]
                parts.append(split(jnp.where(valid, row, 0.0), splits))
            left.append(jnp.concatenate([masked_rows(mask, parts[r][s]) for s in range(splits) for r in range(3)], axis=0))
            right.append(one_hot(index & (LANES - 1), LANES))
    returned = contract_lanes(jnp.concatenate(left, axis=1), jnp.concatenate(right, axis=1))
    free = jnp.where(mask_ref[...] == 0, step_size, 0.0)
    moved = []
    for r in range(3):
        added = sum(returned[i * owned_rows : (i + 1) * owned_rows] for i in range(r, 3 * splits, 3))
        here = jnp.concatenate(
            [positions_ref[r : r + 1, h * LANES : (h + 1) * LANES] for h in range(owned_rows)], axis=0
        )
        moved.append(here - free * (own_ref[r] + added))
    return moved


def move_kernel(positions_ref, mask_ref, own_ref, back_ref, list_ref, valid_ref, *out_refs, dom_count, splits):
    moved = moved_positions(positions_ref, mask_ref, own_ref, back_ref, list_ref, valid_ref, dom_count, splits)
    owned_rows = own_ref.shape[1]
    for r in range(3):
        for h in range(owned_rows):
            out_refs[0][r : r + 1, h * LANES : (h + 1) * LANES] = moved[r][h : h + 1]
    if len(out_refs) > 1:
        out_refs[1][...] = jnp.zeros(out_refs[1].shape, jnp.float32)
        write_payload(lambda r, h: moved[r][h : h + 1], owned_rows, list_ref, valid_ref, out_refs[1], dom_count)


def per_device(positions, fixed_mask, send_count, send_list, block_nodes, tet_corners):
    node_count = positions.shape[1]
    slot_count, sub_count, width = send_list.shape[2:]
    dom_count = lax.axis_size("dom")
    block_count = block_nodes.shape[1]
    owned_rows = node_count // LANES
    counts = send_count[0, 0].T
    lists = send_list[0, 0]
    mask_rows = fixed_mask.reshape(owned_rows, LANES)
    corners = tet_corners.reshape(4, block_count, LANES).transpose(1, 0, 2)

    vmem = pl.BlockSpec(memory_space=pltpu.VMEM)
    hbm = pl.BlockSpec(memory_space=pl.ANY)
    exchange_shape = jax.ShapeDtypeStruct((dom_count * sub_count, 1, 3 * LANES), jnp.float32)
    position_shape = jax.ShapeDtypeStruct(positions.shape, jnp.float32)
    params = pltpu.CompilerParams(vmem_limit_bytes=32 * 1024 * 1024)

    def call(kernel, name, ins, outs, scratch=(), **sizes):
        return pl.pallas_call(
            functools.partial(kernel, **sizes),
            out_shape=outs,
            in_specs=ins,
            out_specs=jax.tree.map(lambda _: vmem, outs),
            scratch_shapes=scratch,
            compiler_params=params,
            name=name,
        )

    send = call(
        send_kernel,
        "send",
        [hbm] * 5,
        (
            exchange_shape,
            jax.ShapeDtypeStruct(lists.shape, jnp.float32),
            jax.ShapeDtypeStruct((block_count // 2, LANES), jnp.int32),
            jax.ShapeDtypeStruct(block_nodes.shape, jnp.int32),
            jax.ShapeDtypeStruct(corners.shape, jnp.int32),
        ),
        [
            pltpu.VMEM(positions.shape, jnp.float32),
            pltpu.VMEM(lists.shape, jnp.int32),
            pltpu.VMEM(counts.shape, jnp.int32),
            pltpu.SemaphoreType.DMA((5,)),
        ],
        dom_count=dom_count,
    )
    own_shape = jax.ShapeDtypeStruct((3, owned_rows, LANES), jnp.float32)

    def exchange(rows):
        return lax.all_to_all(rows, ("dom", "sub"), 0, 0, tiled=True)

    inputs = (positions, lists, counts, block_nodes, corners)
    payload, valid, pair_nodes, block_nodes, corners = send(*[pltpu.with_memory_space_constraint(x, pltpu.HBM) for x in inputs])
    for step in range(ITERS):
        last = step == ITERS - 1
        ghosts = exchange(payload)
        splits = 2 if last else 3
        gradient = call(
            gradient_kernel,
            "gradient_last" if last else "gradient",
            [vmem] * 5,
            (own_shape, exchange_shape),
            [
                pltpu.VMEM((6, block_count * (4 if last else 8), LANES), jnp.float32),
                pltpu.VMEM((block_count * 4, LANES), jnp.float32),
            ],
            dom_count=dom_count,
            slot_count=slot_count,
            splits=splits,
        )
        own, back = gradient(positions, ghosts, pair_nodes, block_nodes, corners)
        returned = exchange(back)
        move = call(
            move_kernel,
            "move_last" if last else "move",
            [vmem] * 6,
            (position_shape,) if last else (position_shape, exchange_shape),
            dom_count=dom_count,
            splits=splits,
        )
        moved = move(positions, mask_rows, own, returned, lists, valid)
        positions = moved[0]
        if not last:
            payload = moved[1]
    return positions


def solution(mesh):
    return jax.shard_map(
        per_device,
        mesh=mesh,
        in_specs=(
            P(None, ("dom", "sub")),
            P(("dom", "sub")),
            P("dom", "sub", None, None),
            P("dom", "sub", None, None, None),
            P(None, ("dom", "sub")),
            P(None, ("dom", "sub")),
        ),
        out_specs=P(None, ("dom", "sub")),
        check_vma=False,
    )
```
